256 devices in a mesh: ctx: 32 (over z, y_lo, core), exp: 8 (over x, y_hi).
Axes of the slice: x: 4, y: 4 (y_hi: 2, y_lo: 2; y = y_hi * 2 + y_lo), z: 8, core: 2. Of those that a mesh axis runs over, the one named last changes fastest.
Arguments:
- hidden_in: bfloat16 [512, 6144], P(None, 'ctx'), may hold values from -4 to 4
- queries: bfloat16 [512, 6144], P(None, 'exp'), may hold values from -48 to 48
- keys: bfloat16 [16384, 1024], P('ctx', 'exp'), may hold values from -24 to 24
- values: bfloat16 [16384, 1024], P('ctx', 'exp'), may hold values from -6 to 6
- out_weight: bfloat16 [6144, 6144], P('exp', 'ctx'), may hold values from -0.078125 to 0.078125
- norm_gain: float32 [6144], replicated, may hold values from 0.25 to 1.75
- expert_gate: bfloat16 [8, 6144, 8192], P('exp', None, 'ctx'), may hold values from -0.078125 to 0.078125
- expert_up: bfloat16 [8, 6144, 8192], P('exp', None, 'ctx'), may hold values from -0.078125 to 0.078125
- expert_down: bfloat16 [8, 8192, 6144], P('exp', 'ctx'), may hold values from -0.125 to 0.125
- expert_ids: int32 [512, 2], replicated, may hold values from 0 to 7, all different within a row; in each aligned block of 512 rows (0 to 511, 512 to 1023, ...) at most 256 rows name the same one
- route_weights: float32 [512, 2], replicated, may hold values from 0.2 to 1
Outputs:
- mixed: bfloat16 [512, 6144], P('exp', 'ctx')
The draws below stay inside these ranges and needn't reach their ends.
Inputs may be any that keep to these rules, and one draw needn't show every extreme that they name: `expert_ids`: the two experts of a token differ; no expert is named by more than 256 tokens of the slab, a bound that some block reaches.
All inputs are finite; a program needn't handle non-finite values.
Results may differ from the reference program's by a relative error of at most 0.03.
Values may be sent and summed in bfloat16 or wider, within the bound.
A program may use at most 192 MiB of HBM per device.

```python
import math
import jax
import jax.numpy as jnp
import numpy as np
from jax import lax

D = 6144
HD = 128
QH_DEV = 6
TOPK = 2
FF_WIN = 8192
Q = 512
CONTEXT = 16384
KV_HEADS = 8
HEADS = 48
EXPERTS = 8
CAP = 256


def key_table(key):
    base_keys = jax.random.normal(key, (CONTEXT, KV_HEADS * HD), jnp.float32)
    return base_keys


def draw_keys(key, part):
    base_keys = key_table(key)
    return base_keys.astype(jnp.bfloat16)


def draw_queries(key, part):
    key = jax.random.fold_in(key, 5)
    drawn = 2.5 * jax.random.normal(key, (Q, HEADS * HD), jnp.float32)
    return drawn.astype(jnp.bfloat16)


def raised(result, key, source, target, blocks, factor):
    def block_of(dim):
        return (jnp.arange(result.shape[dim]) // (result.shape[dim] // blocks)).reshape((-1,) + (1,) * (result.ndim - 1 - dim))

    one_side = jax.random.permutation(key, blocks)[block_of(target)]
    second = (block_of(target) + blocks // 2) % blocks
    return jnp.where((block_of(source) == one_side) | (block_of(source) == second), factor * result, result)


def block_levels(stream_key, shape, split, low, high):
    def one(axis_at, parts):
        steps = jax.random.uniform(jax.random.fold_in(jax.random.fold_in(stream_key, 6), axis_at), (parts,), jnp.float32, low / len(split), high / len(split))
        return jnp.repeat(jnp.exp(steps), shape[axis_at] // parts).reshape((-1,) + (1,) * (len(shape) - axis_at - 1))

    loudness = one(*split[0])
    for cut in split[1:]:
        loudness = loudness * one(*cut)
    return loudness


def routed_block(rng, own, number, rows, count, top, most, skew):
    order = jax.random.permutation(rng, count)
    crowded, ordinary = shares(count, rows * top, most, skew, True), shares(count, rows * top, most, skew, False)
    places = jnp.arange(count)

    def named(sizes, offset_by):
        used = int((sizes > 0).sum())
        fixed = max(1, used // 4)
        passed = fixed + (places - fixed + offset_by * (used - fixed)) % max(1, count - fixed)
        return jnp.zeros((count,), jnp.int32).at[order[jnp.where(places < fixed, places, passed)]].set(jnp.asarray(sizes, jnp.int32))

    sizes = jnp.where(number % 4 == 0, named(crowded, number // 4), named(ordinary, number - number // 4 - 1))
    mixed = jax.random.permutation(jax.random.fold_in(own, 3), count)
    source_of, receiver = mixed[0:count // 2 * 2:2], mixed[1:count // 2 * 2:2]
    margin = jnp.minimum(sizes[source_of] - 1, most - sizes[receiver]) // 2
    margin = jnp.where((source_of == order[0]) | (receiver == order[0]) | (sizes[receiver] == 0), 0, jnp.maximum(margin, 0))
    passed = jax.random.randint(jax.random.fold_in(own, 4), (count // 2,), 0, 1 << 20) % (margin + 1)
    sizes = sizes.at[source_of].add(-passed).at[receiver].add(passed)
    labels = jnp.searchsorted(jnp.cumsum(sizes), jnp.arange(rows * top), side="right").astype(jnp.int32)
    grid = labels.reshape(top, rows).T
    grid = grid[jax.random.permutation(jax.random.fold_in(own, 1), rows)]
    offset_by = jax.random.randint(jax.random.fold_in(own, 2), (rows, 1), 0, top)
    return jnp.take_along_axis(grid, (jnp.arange(top)[None, :] + offset_by) % top, axis=1)


def shares(number_of, total, bound, slope, full):
    portions = [(1 << 20) // math.isqrt(standing ** slope) + 1 for standing in range(1, number_of + 1)]
    largest = bound if full else min(bound, max(-(-total // number_of), total * portions[0] // sum(portions)))
    least = 1 if total - largest >= number_of - 1 else 0
    counts, rest = [largest] + [least] * (number_of - 1), total - largest - least * (number_of - 1)
    while rest > 0:
        free = [i for i in range(1, number_of) if counts[i] < largest] or [i for i in range(1, number_of) if counts[i] < bound]
        whole, remaining = sum([portions[i] for i in free]), rest
        for i in free:
            addition = min(bound - counts[i], max(1, remaining * portions[i] // whole), rest)
            counts[i] = counts[i] + addition
            rest = rest - addition
    return np.array(counts)


def noise(key, dims, spread, limit, split=(), kind=jnp.bfloat16):
    level = block_levels(key, dims, split, -0.22, 0.18) if split else 1.0
    values = jax.random.normal(key, dims, jnp.float32) * spread * level
    return jnp.minimum(jnp.maximum(values, -limit), limit).astype(kind)


def heavy_noise(rng, dims, width, limit, shards, heavy, held_as=jnp.bfloat16):
    values = width * jax.random.normal(rng, dims, jnp.float32)
    if shards:
        values = values * block_levels(rng, dims, shards, -0.22, 0.18)
    return jnp.clip(raised(values, jax.random.fold_in(rng, 3), *heavy), -limit, limit).astype(held_as)


def setup_inputs(seed: int = 0) -> dict:
    splits = jax.random.split(jax.random.key(seed), 12)
    hidden_in = noise(splits[0], (Q, D), 0.5, 4.0, ((1, 32),))
    queries = draw_queries(jax.random.fold_in(splits[11], 71), 0)
    keys = draw_keys(jax.random.fold_in(splits[11], 71), 0)
    values = noise(splits[3], (CONTEXT, KV_HEADS * HD), 1.0, 6.0, ((0, 32), (1, 8)))
    out_weight = noise(splits[4], (HEADS * HD, D), (HEADS * HD) ** -0.5, 0.078125, ((0, 8), (1, 32)))
    norm_gain = jnp.clip(1.0 + 0.15 * jax.random.normal(splits[5], (D,), jnp.float32), 0.25, 1.75)
    expert_gate = noise(splits[6], (EXPERTS, D, FF_WIN), D ** -0.5, 0.078125, ((0, 8), (2, 32)))
    expert_up = noise(splits[7], (EXPERTS, D, FF_WIN), D ** -0.5, 0.078125, ((0, 8), (2, 32)))
    expert_down = heavy_noise(splits[8], (EXPERTS, FF_WIN, D), FF_WIN ** -0.5, 0.125, ((0, 8), (1, 32)), (1, 2, 32, 2.75))
    expert_ids_keys = jax.random.split(jax.random.fold_in(splits[9], 1), Q // Q)
    expert_ids_turns = jax.random.permutation(jax.random.fold_in(splits[9], 3), Q // Q)
    expert_ids = jax.vmap(lambda own, number: routed_block(jax.random.fold_in(splits[9], 2), own, number, Q, EXPERTS, TOPK, CAP, 2))(expert_ids_keys, expert_ids_turns).reshape((Q, TOPK))
    route_weights = jnp.clip(jax.random.uniform(splits[10], (Q, TOPK), jnp.float32, 0.2, 1.0), 0.2, 1.0)
    return {"hidden_in": hidden_in, "queries": queries, "keys": keys, "values": values, "out_weight": out_weight, "norm_gain": norm_gain, "expert_gate": expert_gate, "expert_up": expert_up, "expert_down": expert_down, "expert_ids": expert_ids, "route_weights": route_weights}


def attend_group(operands):
    group_queries, group_keys, group_values = operands
    scores = jnp.einsum('qhd,kd->hqk', group_queries.astype(jnp.float32), group_keys.astype(jnp.float32)) * (1.0 / math.sqrt(HD))
    query_pos = CONTEXT - Q + jnp.arange(Q, dtype=jnp.int32)
    key_pos = jnp.arange(CONTEXT, dtype=jnp.int32)
    visible = key_pos[None, :] <= query_pos[:, None]
    scores = jnp.where(visible[None], scores, -1e+30)
    peak = lax.optimization_barrier(jnp.max(scores, axis=-1, keepdims=True))
    weights = jnp.exp(scores - peak)
    totals = lax.optimization_barrier(jnp.sum(weights, axis=-1))
    rounded = lax.optimization_barrier(weights.astype(jnp.bfloat16)).astype(jnp.float32)
    numer = jnp.einsum('hqk,kd->qhd', rounded, group_values.astype(jnp.float32))
    return (numer / jnp.transpose(totals)[:, :, None]).astype(jnp.bfloat16)

def reference(hidden_in, queries, keys, values, out_weight, norm_gain, expert_gate, expert_up, expert_down, expert_ids, route_weights):
    queries_grouped = queries.reshape(Q, KV_HEADS, QH_DEV, HD).transpose(1, 0, 2, 3)
    keys_grouped = keys.reshape(CONTEXT, KV_HEADS, HD).transpose(1, 0, 2)
    values_grouped = values.reshape(CONTEXT, KV_HEADS, HD).transpose(1, 0, 2)
    attended = lax.map(attend_group, (queries_grouped, keys_grouped, values_grouped))
    attended = attended.transpose(1, 0, 2, 3).reshape(Q, KV_HEADS * QH_DEV * HD)
    projected = jnp.dot(attended, out_weight, preferred_element_type=jnp.float32)
    stream = (hidden_in.astype(jnp.float32) + projected).astype(jnp.bfloat16)
    stream_full = stream.astype(jnp.float32)
    inverse_rms = lax.rsqrt(lax.optimization_barrier(jnp.mean(stream_full * stream_full, axis=-1)) + 1e-05)
    scaled = (stream_full * norm_gain).astype(jnp.bfloat16)

    def expert_step(running, operands):
        gate_w, up_w, down_w, expert = operands
        gate_val = jnp.dot(scaled, gate_w, preferred_element_type=jnp.float32) * inverse_rms[:, None]
        up_val = jnp.dot(scaled, up_w, preferred_element_type=jnp.float32) * inverse_rms[:, None]
        hidden = (jax.nn.silu(gate_val) * up_val).astype(jnp.bfloat16)
        expert_out = jnp.dot(hidden, down_w, preferred_element_type=jnp.float32)
        weight = lax.optimization_barrier(jnp.sum(jnp.where(expert_ids == expert, route_weights, jnp.zeros_like(route_weights)), axis=1))
        return (running + weight[:, None] * expert_out, None)
    running, _ = lax.scan(expert_step, jnp.zeros((Q, D), jnp.float32), (expert_gate, expert_up, expert_down, jnp.arange(EXPERTS, dtype=jnp.int32)))
    return (stream_full + running).astype(jnp.bfloat16)
```

```python
import math

import jax
import jax.numpy as jnp
from jax import lax
from jax.experimental import pallas as pl
from jax.experimental.pallas import tpu as pltpu
from jax.sharding import PartitionSpec as P

F32 = jnp.float32
BF16 = jnp.bfloat16
MESH = pl.DeviceIdType.MESH

HD = 128
D = 6144
Q = 512
CONTEXT = 16384
CHIPS = 16
ZN = 8
EN = 8
HEADS = 6
HALF = Q // 2
ROWS = HALF // CHIPS
PAIRS = ROWS * HEADS
BLK = 512
WIDE = 384
COLS = 192
SLOTS = 256
SH = SLOTS // 2
SQ = SH // 2
TOKB = HALF // EN
OUTR = Q // EN
FF = 256
MSG = PAIRS + 16
FAR = (8, 7, 9, 6, 10, 5, 11, 4, 12, 3, 13, 2, 14, 1, 15, 0)
GROUP = 4


def dot(a, b, dims=((1,), (0,))):
    return lax.dot_general(a, b, (dims, ((), ())), preferred_element_type=F32)


def iota(shape, dim):
    return lax.broadcasted_iota(jnp.int32, shape, dim)


def one_hot_columns(shape, shift, along):
    other = 1 - along
    return jnp.where(iota(shape, along) == iota(shape, other) + shift, 1.0, 0.0).astype(BF16)


def layer_kernel(
    ids_ref, rw_ref, gain_ref, q_hbm, k_hbm, v_hbm, hin_hbm, wout_hbm, gate_hbm, up_hbm, down_hbm,
    out_ref,
    q_s, k_s, v_s, h_s, w_s, wc_s, gate_s, up_s, down_s,
    num_s, got_s, own_s, att_s, ps_s, pr_s, own_p, st_s,
    xs_s, xr_s, x_s, acc_s, sq_s, part_s, ys_s, yr_s,
    h1rs, h1rr, h1ls, h1lr, h2rs, h2rr, h2ls, h2lr, f1s, f1r,
    o_s, os_s, or_s, rs_s, rr_s, ts_s, tr_s, town_s, tok_s,
    lsem, ssem, rsem, asem, arsem, bsem, brsem, psem, prsem, gsem, grsem, tsem, trsem,
    ysem, yrsem, xsem, xrsem, esem, ersem,
):
    c = lax.axis_index("ctx")
    e = lax.axis_index("exp")
    core = c % 2
    chip = c // 2
    y = chip % 2
    z = chip // 2
    sib = c + 1 - 2 * core
    ypeer = c + 2 - 4 * y
    right = ((z + 1) % ZN) * 4 + y * 2 + core
    left = ((z + ZN - 1) % ZN) * 4 + y * 2 + core

    def remote(src, dst, send, recv, ctx=None, ex=None):
        return pltpu.make_async_remote_copy(
            src_ref=src, dst_ref=dst, send_sem=send, recv_sem=recv,
            device_id=(c if ctx is None else ctx, e if ex is None else ex),
            device_id_type=MESH,
        )

    def arrived(ref, sem):
        pltpu.make_async_copy(ref, ref, sem).wait()

    sent = []

    def push(*args, **kw):
        copy = remote(*args, **kw)
        copy.start()
        sent.append(copy)

    barrier = pltpu.get_barrier_semaphore()

    def greet(ctx, ex):
        pl.semaphore_signal(barrier, inc=1, device_id=(ctx, ex), device_id_type=MESH)

    greet(sib, e)
    for d in range(1, CHIPS):
        greet(2 * ((chip + d) % CHIPS) + core, e)
    for d in range(1, EN):
        greet(c, (e + d) % EN)

    half_rows = pl.ds(pl.multiple_of(HALF * core, HALF), HALF)
    my_rows = pl.ds(pl.multiple_of(HALF * core + TOKB * e, TOKB), TOKB)
    sib_rows = pl.ds(pl.multiple_of(HALF * (1 - core) + TOKB * e, TOKB), TOKB)
    gate_h, up_h, down_h = gate_hbm.at[0], up_hbm.at[0], down_hbm.at[0]
    loads = [
        pltpu.make_async_copy(q_hbm.at[half_rows, :], q_s, lsem.at[0]),
        pltpu.make_async_copy(k_hbm, k_s.at[core], lsem.at[1]),
        pltpu.make_async_copy(v_hbm, v_s.at[core], lsem.at[2]),
        pltpu.make_async_copy(hin_hbm.at[my_rows, :], h_s.at[core], lsem.at[3]),
        pltpu.make_async_copy(wout_hbm, w_s.at[core], lsem.at[4]),
        pltpu.make_async_copy(gate_h, gate_s.at[core], lsem.at[5]),
        pltpu.make_async_copy(up_h, up_s.at[core], lsem.at[6]),
        pltpu.make_async_copy(down_h, down_s.at[core], lsem.at[7]),
    ]
    for load in loads[:5]:
        load.start()

    pl.semaphore_wait(barrier, 1 + (CHIPS - 1) + (EN - 1))

    push(k_hbm, k_s.at[core], ssem.at[0], rsem.at[0], ctx=sib)
    push(v_hbm, v_s.at[core], ssem.at[1], rsem.at[1], ctx=sib)
    push(hin_hbm.at[sib_rows, :], h_s.at[core], ssem.at[2], rsem.at[2], ctx=sib)
    push(wout_hbm, w_s.at[core], ssem.at[3], rsem.at[3], ctx=sib)
    for load in loads[5:]:
        load.start()
    push(gate_h, gate_s.at[core], ssem.at[4], rsem.at[4], ctx=sib)
    push(up_h, up_s.at[core], ssem.at[5], rsem.at[5], ctx=sib)
    push(down_h, down_s.at[core], ssem.at[6], rsem.at[6], ctx=sib)

    loads[0].wait()
    loads[1].wait()
    arrived(k_s.at[1 - core], rsem.at[0])
    loads[2].wait()
    arrived(v_s.at[1 - core], rsem.at[1])
    keys = k_s[...].reshape(2 * BLK, HD)
    vals = jnp.concatenate([v_s[...].reshape(2 * BLK, HD), jnp.ones((2 * BLK, HD), BF16)], axis=1)
    diag = iota((PAIRS, HD), 0) == iota((PAIRS, HD), 1)
    stat_row = iota((16, HD), 0)
    first_limit = CONTEXT - Q + HALF * core - 2 * BLK * chip
    for start in range(0, CHIPS, GROUP):
        owners = [(chip + d) % CHIPS for d in FAR[start : start + GROUP]]
        rows, limits = [], []
        for p in owners:
            at = pl.ds(pl.multiple_of(ROWS * p, ROWS), ROWS)
            for h in range(HEADS):
                rows.append(q_s[at, HD * h : HD * (h + 1)])
                limits.append(iota((ROWS, 1), 0) + (first_limit + ROWS * p))
        qg = jnp.concatenate(rows, axis=0)
        limit = jnp.concatenate(limits, axis=0)
        scores = dot(qg, keys, ((1,), (1,))) * (math.log2(math.e) / math.sqrt(HD))
        scores = jnp.where(iota(scores.shape, 1) <= limit, scores, -1e30)
        peak = jnp.max(scores, axis=1, keepdims=True)
        weights = jnp.exp2(scores - peak).astype(BF16)
        both = dot(weights, vals)
        total = both[:, HD:]
        numer = (both[:, :HD] / total).astype(BF16)
        peaks = jnp.broadcast_to(peak, total.shape)
        for g, p in enumerate(owners):
            part = slice(PAIRS * g, PAIRS * (g + 1))
            pk = jnp.sum(jnp.where(diag, peaks[part], 0.0), axis=0, keepdims=True)
            tt = jnp.sum(jnp.where(diag, total[part], 0.0), axis=0, keepdims=True)
            pk0 = pk.astype(BF16).astype(F32)
            pk1 = (pk - pk0).astype(BF16).astype(F32)
            pk2 = pk - pk0 - pk1
            tt0 = tt.astype(BF16).astype(F32)
            stats = jnp.where(stat_row == 0, pk0, 0.0)
            for at, term in ((1, pk1), (2, pk2), (3, tt0), (4, tt - tt0)):
                stats = jnp.where(stat_row == at, term, stats)
            d = FAR[start + g]
            if d:
                num_s[p, :PAIRS, :] = numer[part]
                num_s[p, PAIRS:, :] = stats.astype(BF16)
                push(num_s.at[p], got_s.at[chip], asem.at[d], arsem.at[chip], ctx=2 * p + core)
            else:
                own_s[:PAIRS, :] = numer[part]
                own_s[PAIRS:, :] = stats.astype(BF16)

    ids = ids_ref[...]
    owned = jnp.where((ids[0:1] == e) | (ids[1:2] == e), 1.0, 0.0)
    w_row = jnp.where(ids[0:1] == e, rw_ref[0:1, :], 0.0) + jnp.where(ids[1:2] == e, rw_ref[1:2, :], 0.0)
    before = jnp.where(iota((Q, Q), 0) < iota((Q, Q), 1), 1.0, 0.0).astype(BF16)
    rank = dot(jnp.broadcast_to(owned, (16, Q)).astype(BF16), before)[0:1]
    place = jnp.where(owned > 0.5, rank, -1.0)
    place_col = jnp.transpose(jnp.broadcast_to(place, (HD, Q)))
    for part in range(2):
        lane = (iota((Q, SH), 1) + SH * part).astype(F32)
        tok_s[:, SH * part : SH * (part + 1)] = jnp.where(place_col == lane, 1.0, 0.0).astype(BF16)
    slot_own = (iota((SH, Q), 0) + SH * core).astype(F32)
    w_slot = jnp.sum(jnp.where(place == slot_own, w_row, 0.0), axis=1, keepdims=True)

    spread = [one_hot_columns((COLS, WIDE), COLS * at, 1) for at in range(2)]
    loads[4].wait()
    arrived(w_s.at[1 - core], rsem.at[3])
    wc_s[...] = (dot(w_s[0], spread[0]) + dot(w_s[1], spread[1])).astype(BF16)

    peaks, totals, numers = [], [], []
    for d in range(CHIPS):
        source = (chip + d) % CHIPS
        block = own_s if d == 0 else got_s.at[source]
        if d:
            arrived(block, arsem.at[source])
        stats = block[PAIRS:, :].astype(F32)
        peaks.append(stats[0:1] + stats[1:2] + stats[2:3])
        totals.append(stats[3:4] + stats[4:5])
    top = peaks[0]
    for pk in peaks[1:]:
        top = jnp.maximum(top, pk)
    factors = [jnp.exp2(pk - top) * tt for pk, tt in zip(peaks, totals)]
    whole = factors[0]
    for f in factors[1:]:
        whole = whole + f
    inverse = 1.0 / jnp.maximum(whole, 1e-30)
    merged = jnp.zeros((PAIRS, HD), F32)
    for d in range(CHIPS):
        source = (chip + d) % CHIPS
        block = own_s if d == 0 else got_s.at[source]
        column = jnp.sum(jnp.where(diag, factors[d] * inverse, 0.0), axis=1, keepdims=True)
        merged = merged + column * block[:PAIRS, :].astype(F32)
    att_s[chip] = merged.astype(BF16)
    for d in FAR[:-1]:
        push(att_s.at[chip], att_s.at[chip], bsem.at[d], brsem.at[chip], ctx=2 * ((chip + d) % CHIPS) + core)
    for d in range(1, CHIPS):
        source = (chip + d) % CHIPS
        arrived(att_s.at[source], brsem.at[source])

    attended = jnp.concatenate(
        [att_s[:, ROWS * h : ROWS * (h + 1), :].reshape(HALF, HD) for h in range(HEADS)], axis=1
    )
    projected = dot(attended, wc_s[...])
    own_p[...] = projected
    ps_s[...] = projected.astype(BF16).reshape(EN, TOKB, WIDE)
    for d in range(1, EN):
        to = (e + d) % EN
        push(ps_s.at[to], pr_s.at[e], psem.at[d], prsem.at[e], ex=to)
    loads[3].wait()
    arrived(h_s.at[1 - core], rsem.at[2])
    stream = own_p[pl.ds(pl.multiple_of(TOKB * e, TOKB), TOKB), :]
    for d in range(1, EN):
        source = (e + d) % EN
        arrived(pr_s.at[source], prsem.at[source])
        stream = stream + pr_s[source].astype(F32)
    stream = stream + (dot(h_s[0], spread[0]) + dot(h_s[1], spread[1]))
    st_s[e] = stream.astype(BF16)
    for d in range(1, EN):
        to = (e + d) % EN
        push(st_s.at[e], st_s.at[e], gsem.at[d], grsem.at[e], ex=to)
    for d in range(1, EN):
        source = (e + d) % EN
        arrived(st_s.at[source], grsem.at[source])

    rows = st_s[...].reshape(HALF, WIDE)

    def slots_of(part):
        token = iota((SH, HALF), 1) + HALF * core
        pick = iota((SH, HALF), 0) + SH * part
        here = jnp.where(core == 0, place[:, :HALF], place[:, HALF:])
        hot = jnp.where(here == pick.astype(F32), 1.0, 0.0).astype(BF16)
        return dot(hot, rows)

    xs_s[...] = slots_of(1 - core).astype(BF16)
    push(xs_s, xr_s, ssem.at[7], rsem.at[7], ctx=sib)
    resid = st_s[pl.ds(2 * (e % 4), 2)].reshape(OUTR, WIDE)
    take_own = jnp.where(iota((WIDE, 256), 0) == iota((WIDE, 256), 1) + COLS * core, 1.0, 0.0)
    take_sib = jnp.where(iota((WIDE, 256), 0) == iota((WIDE, 256), 1) + COLS * (1 - core), 1.0, 0.0)
    valid = iota((WIDE, 256), 1) < COLS
    take_own = jnp.where(valid, take_own, 0.0).astype(BF16)
    take_sib = jnp.where(valid, take_sib, 0.0).astype(BF16)
    rs_s[...] = dot(resid, take_sib).astype(BF16)
    push(rs_s, rr_s, ssem.at[8], rsem.at[8], ctx=sib)
    resid_own = dot(resid, take_own)
    mine = slots_of(core)
    arrived(xr_s, rsem.at[7])
    x_s[z, y] = (mine + xr_s[...].astype(F32)).astype(BF16)

    top_half, low_half = pl.ds(0, SQ), pl.ds(SQ, SQ)
    zp = [(z + d) % ZN for d in range(ZN)]

    def near(d):
        return zp[d % ZN]

    def x_low(d, yy):
        return x_s.at[near(d), yy, low_half, :]

    def x_top(d):
        return x_s.at[near(d), :, top_half, :]

    own_top = x_s.at[z, y, top_half, :]
    push(own_top, own_top, xsem.at[0], xrsem.at[0], ctx=ypeer)
    push(x_low(0, y), x_low(0, y), xsem.at[8], xrsem.at[8], ctx=right)
    push(x_low(0, y), x_low(0, y), xsem.at[11], xrsem.at[11], ctx=left)
    push(x_low(0, y), x_low(0, y), tsem.at[0], trsem.at[z], ctx=ypeer)
    arrived(x_s.at[z, 1 - y, top_half, :], xrsem.at[0])
    push(x_top(0), x_top(0), xsem.at[1], xrsem.at[1], ctx=right)
    push(x_top(0), x_top(0), xsem.at[5], xrsem.at[5], ctx=left)

    loads[5].wait()
    loads[6].wait()
    arrived(gate_s.at[1 - core], rsem.at[4])
    arrived(up_s.at[1 - core], rsem.at[5])
    acc_s[...] = jnp.zeros_like(acc_s)
    sq_s[...] = jnp.zeros_like(sq_s)

    def project(d):
        zz = near(d)
        for yy in range(2):
            at = pl.ds(pl.multiple_of(WIDE * (2 * zz + yy), WIDE), WIDE)
            block = x_s[zz, yy].astype(F32)
            square = block * block
            sq_s[...] += square[:, :128] + square[:, 128:256] + square[:, 256:]
            scaled = (block * gain_ref[:, at]).astype(BF16)
            for kk in range(2):
                acc_s[0, kk] += dot(scaled, gate_s[kk, at, :])
                acc_s[1, kk] += dot(scaled, up_s[kk, at, :])

    def low_arrived(d):
        arrived(x_low(d, 1 - y), trsem.at[near(d)])

    for s in range(1, 5):
        if s <= 3:
            arrived(x_low(-s, y), xrsem.at[7 + s])
            if s < 3:
                push(x_low(-s, y), x_low(-s, y), xsem.at[8 + s], xrsem.at[8 + s], ctx=right)
            push(x_low(-s, y), x_low(-s, y), tsem.at[ZN - s], trsem.at[near(-s)], ctx=ypeer)
        arrived(x_low(s, y), xrsem.at[10 + s])
        if s < 4:
            push(x_low(s, y), x_low(s, y), xsem.at[11 + s], xrsem.at[11 + s], ctx=left)
        push(x_low(s, y), x_low(s, y), tsem.at[s], trsem.at[near(s)], ctx=ypeer)
        arrived(x_top(-s), xrsem.at[s])
        if s < 4:
            push(x_top(-s), x_top(-s), xsem.at[1 + s], xrsem.at[1 + s], ctx=right)
        if s <= 3:
            arrived(x_top(s), xrsem.at[4 + s])
            if s < 3:
                push(x_top(s), x_top(s), xsem.at[5 + s], xrsem.at[5 + s], ctx=left)
        if s == 1:
            low_arrived(0)
            project(0)
        else:
            low_arrived(s - 1)
            project(s - 1)
            low_arrived(1 - s)
            project(1 - s)
    low_arrived(4)
    project(4)

    inverse_rms = lax.rsqrt(jnp.sum(sq_s[...], axis=1, keepdims=True) / D + 1e-5)
    hidden = []
    for kk in range(2):
        gate_val = acc_s[0, kk] * inverse_rms
        up_val = acc_s[1, kk] * inverse_rms
        hidden.append((gate_val / (1.0 + jnp.exp(-gate_val)) * up_val).astype(BF16))
    loads[7].wait()
    arrived(down_s.at[1 - core], rsem.at[6])

    def expand(d):
        zz = near(d)
        for yy in range(2):
            at = pl.ds(pl.multiple_of(WIDE * (2 * zz + yy), WIDE), WIDE)
            part_s[zz, yy] = dot(hidden[0], down_s[0, :, at]) + dot(hidden[1], down_s[1, :, at])
        ys_s[zz] = part_s[zz, 1 - y, SQ:, :].astype(BF16)
        push(ys_s.at[zz], yr_s.at[zz], ysem.at[d % ZN], yrsem.at[zz], ctx=ypeer)

    def top_right(s):
        d = 4 - s
        value = part_s[near(d), :, :SQ, :]
        if s:
            arrived(h1rr.at[s - 1], esem_r(0, s - 1))
            value = value + h1rr[s - 1].astype(F32)
        h1rs[s] = value.astype(BF16)
        push(h1rs.at[s], h1rr.at[s], esem.at[s], ersem.at[s], ctx=right)

    def esem_r(kind, s):
        return ersem.at[4 * kind + s]

    def top_left(s):
        d = s - 3
        value = part_s[near(d), :, :SQ, :]
        if s:
            arrived(h1lr.at[s - 1], esem_r(1, s - 1))
            value = value + h1lr[s - 1].astype(F32)
        h1ls[s] = value.astype(BF16)
        push(h1ls.at[s], h1lr.at[s], esem.at[4 + s], esem_r(1, s), ctx=left)

    def low_value(d):
        arrived(yr_s.at[near(d)], yrsem.at[near(d)])
        return part_s[near(d), y, SQ:, :] + yr_s[near(d)].astype(F32)

    def low_right(s):
        value = low_value(3 - s)
        if s:
            arrived(h2rr.at[s - 1], esem_r(2, s - 1))
            value = value + h2rr[s - 1].astype(F32)
        h2rs[s] = value.astype(BF16)
        push(h2rs.at[s], h2rr.at[s], esem.at[8 + s], esem_r(2, s), ctx=right)

    def low_left(s):
        value = low_value(s - 4)
        if s:
            arrived(h2lr.at[s - 1], esem_r(3, s - 1))
            value = value + h2lr[s - 1].astype(F32)
        h2ls[s] = value.astype(BF16)
        push(h2ls.at[s], h2lr.at[s], esem.at[12 + s], esem_r(3, s), ctx=left)

    expand(4)
    top_right(0)
    expand(-3)
    top_left(0)
    expand(3)
    expand(-2)
    expand(2)
    expand(-1)
    expand(1)
    expand(0)
    low_left(0)
    low_right(0)
    for s in range(1, 4):
        top_right(s)
        if s < 3:
            top_left(s)
        low_left(s)
        if s < 3:
            low_right(s)
    arrived(h1rr.at[3], esem_r(0, 3))
    arrived(h1lr.at[2], esem_r(1, 2))
    ends = h1rr[3].astype(F32) + h1lr[2].astype(F32)
    top_sum = jnp.where(y == 0, ends[0], ends[1]) + part_s[z, y, :SQ, :]
    f1s[...] = (jnp.where(y == 0, ends[1], ends[0]) + part_s[z, 1 - y, :SQ, :]).astype(BF16)
    push(f1s, f1r, ssem.at[9], rsem.at[9], ctx=ypeer)
    low_sum = low_value(0)
    arrived(h2rr.at[2], esem_r(2, 2))
    arrived(h2lr.at[3], esem_r(3, 3))
    low_sum = low_sum + (h2rr[2].astype(F32) + h2lr[3].astype(F32))
    arrived(f1r, rsem.at[9])
    top_sum = top_sum + f1r[...].astype(F32)
    summed = (jnp.concatenate([top_sum, low_sum], axis=0) * w_slot).astype(BF16)

    os_s[...] = dot(summed, take_sib).astype(BF16)
    push(os_s, or_s, ssem.at[10], rsem.at[10], ctx=sib)
    own_cols = dot(summed, take_own).astype(BF16)
    arrived(or_s, rsem.at[10])
    o_s[core] = own_cols
    o_s[1 - core] = or_s[...]
    slots = o_s[...].reshape(SLOTS, 256)
    town_s[...] = dot(tok_s[...], slots).reshape(EN, OUTR, 256)
    ts_s[...] = town_s[...].astype(BF16)
    for d in range(1, EN):
        to = (e + d) % EN
        push(ts_s.at[to], tr_s.at[e], psem.at[EN + d], prsem.at[EN + e], ex=to)
    arrived(rr_s, rsem.at[8])
    mixed = town_s[e] + jnp.where(core == e // 4, resid_own, rr_s[...].astype(F32))
    for d in range(1, EN):
        source = (e + d) % EN
        arrived(tr_s.at[source], prsem.at[EN + source])
        mixed = mixed + tr_s[source].astype(F32)
    out_ref[...] = mixed[:, :COLS].astype(BF16)
    for copy in sent:
        copy.wait_send()


def local(hidden_in, queries, keys, values, out_weight, norm_gain, expert_gate, expert_up, expert_down, expert_ids, route_weights):
    vmem = pl.BlockSpec(memory_space=pltpu.VMEM)
    anywhere = pl.BlockSpec(memory_space=pl.ANY)
    dma = pltpu.SemaphoreType.DMA

    def buf(*shape, dtype=BF16):
        return pltpu.VMEM(shape, dtype)

    scratch = [
        buf(HALF, HEADS * HD), buf(2, BLK, HD), buf(2, BLK, HD), buf(2, TOKB, COLS),
        buf(2, HEADS * HD, COLS), buf(HEADS * HD, WIDE),
        buf(2, D, FF), buf(2, D, FF), buf(2, FF, D),
        buf(CHIPS, MSG, HD), buf(CHIPS, MSG, HD), buf(MSG, HD), buf(CHIPS, PAIRS, HD),
        buf(EN, TOKB, WIDE), buf(EN, TOKB, WIDE), buf(HALF, WIDE, dtype=F32), buf(EN, TOKB, WIDE),
        buf(SH, WIDE), buf(SH, WIDE), buf(ZN, 2, SH, WIDE),
        buf(2, 2, SH, FF, dtype=F32), buf(SH, 128, dtype=F32), buf(ZN, 2, SH, WIDE, dtype=F32),
        buf(ZN, SQ, WIDE), buf(ZN, SQ, WIDE),
        buf(4, 2, SQ, WIDE), buf(4, 2, SQ, WIDE), buf(3, 2, SQ, WIDE), buf(3, 2, SQ, WIDE),
        buf(3, SQ, WIDE), buf(3, SQ, WIDE), buf(4, SQ, WIDE), buf(4, SQ, WIDE),
        buf(SQ, WIDE), buf(SQ, WIDE),
        buf(2, SH, 256), buf(SH, 256), buf(SH, 256), buf(OUTR, 256), buf(OUTR, 256),
        buf(EN, OUTR, 256), buf(EN, OUTR, 256), buf(EN, OUTR, 256, dtype=F32), buf(Q, SLOTS),
        dma((8,)), dma((11,)), dma((11,)),
        dma((CHIPS,)), dma((CHIPS,)), dma((CHIPS,)), dma((CHIPS,)),
        dma((2 * EN,)), dma((2 * EN,)), dma((EN,)), dma((EN,)), dma((ZN,)), dma((ZN,)),
        dma((ZN,)), dma((ZN,)), dma((15,)), dma((15,)), dma((16,)), dma((16,)),
    ]
    return pl.pallas_call(
        layer_kernel,
        out_shape=jax.ShapeDtypeStruct((OUTR, COLS), BF16),
        in_specs=[vmem] * 3 + [anywhere] * 8,
        out_specs=vmem,
        scratch_shapes=scratch,
        compiler_params=pltpu.CompilerParams(
            collective_id=0, has_side_effects=True, vmem_limit_bytes=56 * 1024 * 1024
        ),
        cost_estimate=pl.CostEstimate(flops=3 * 10**9, bytes_accessed=12 * 10**6, transcendentals=2 * 10**6),
    )(
        expert_ids.T, route_weights.T, norm_gain.reshape(1, D), queries, keys, values, hidden_in,
        out_weight, expert_gate, expert_up, expert_down,
    )


def solution(mesh):
    placed = (
        P(None, "ctx"),
        P(None, "exp"),
        P("ctx", "exp"),
        P("ctx", "exp"),
        P("exp", "ctx"),
        P(),
        P("exp", None, "ctx"),
        P("exp", None, "ctx"),
        P("exp", "ctx", None),
        P(),
        P(),
    )
    return jax.shard_map(
        local, mesh=mesh, in_specs=placed, out_specs=P("exp", "ctx"), check_vma=False
    )
```

```python
import functools
import math

import jax
import jax.numpy as jnp
from jax import lax
from jax.experimental import pallas as pl
from jax.experimental.pallas import tpu as pltpu
from jax.sharding import PartitionSpec as P

F32 = jnp.float32
BF16 = jnp.bfloat16
MESH = pl.DeviceIdType.MESH

HD = 128
D = 6144
Q = 512
CONTEXT = 16384
CHIPS = 16
ZN = 8
EN = 8
HEADS = 6
HALF = Q // 2
ROWS = HALF // CHIPS
PAIRS = ROWS * HEADS
BLK = 512
WIDE = 384
COLS = 192
SLOTS = 256
SH = SLOTS // 2
SQ = SH // 2
TOKB = HALF // EN
OUTR = Q // EN
FF = 256
MSG = PAIRS + 16
FAR = (8, 7, 9, 6, 10, 5, 11, 4, 12, 3, 13, 2, 14, 1, 15, 0)
GROUP = 4
AWAY = (4, -3, 3, -2, 2, -1, 1, 0)


def dot(a, b, dims=((1,), (0,))):
    return lax.dot_general(a, b, (dims, ((), ())), preferred_element_type=F32)


def iota(shape, dim):
    return lax.broadcasted_iota(jnp.int32, shape, dim)


def layer_kernel(
    ids_hbm, rw_hbm, gain_hbm, q_hbm, k_hbm, v_hbm, hin_hbm, wout_hbm, gate_hbm, up_hbm, down_hbm,
    out_ref,
    ids_ref, rw_ref, gain_ref, q_s, k_s, v_s, h_s, w_s, gate_s, up_s, down_s,
    sib_s, sibr_s, part_o, yin_s, num_s, got_s, own_s, att_s, ps_s, pr_s, own_p, st_s,
    xs_s, xr_s, x_s, acc_s, sq_s, part_s, ys_s, yr_s,
    h1rs, h1rr, h1ls, h1lr, h2rs, h2rr, h2ls, h2lr, h2fs, h2fr, f1s, f1r,
    o_s, os_s, or_s, rs_s, rr_s, ts_s, tr_s, town_s, tok_s,
    lsem, ssem, rsem, asem, arsem, bsem, brsem, psem, prsem, gsem, grsem, tsem, trsem,
    ysem, yrsem, xsem, xrsem, esem, ersem, ksem, krsem, vsem, vrsem,
):
    c = lax.axis_index("ctx")
    e = lax.axis_index("exp")
    core = c % 2
    chip = c // 2
    y = chip % 2
    z = chip // 2
    sib = c + 1 - 2 * core
    ypeer = c + 2 - 4 * y
    zp = [(z + d) % ZN for d in range(ZN)]

    def near(d):
        return zp[d % ZN]

    def at_chip(d, yy):
        return near(d) * 4 + yy * 2 + core

    right, left = at_chip(1, y), at_chip(-1, y)

    def owner(i):
        return near(AWAY[i % ZN]) * 2 + (1 - y if i < ZN else y)

    def remote(src, dst, send, recv, ctx=None, ex=None):
        return pltpu.make_async_remote_copy(
            src_ref=src, dst_ref=dst, send_sem=send, recv_sem=recv,
            device_id=(c if ctx is None else ctx, e if ex is None else ex),
            device_id_type=MESH,
        )

    def arrived(ref, sem):
        pltpu.make_async_copy(ref, ref, sem).wait()

    sent = []

    def push(*args, **kw):
        copy = remote(*args, **kw)
        copy.start()
        sent.append(copy)

    def drain(keep=0):
        while len(sent) > keep:
            sent.pop(0).wait_send()

    barrier = pltpu.get_barrier_semaphore()

    def greet(ctx, ex):
        pl.semaphore_signal(barrier, inc=1, device_id=(ctx, ex), device_id_type=MESH)

    greet(sib, e)
    for d in range(1, CHIPS):
        greet(2 * ((chip + d) % CHIPS) + core, e)
    for d in range(1, EN):
        greet(c, (e + d) % EN)

    half_cols = pl.ds(pl.multiple_of(HALF * core, HALF), HALF)
    sib_cols = pl.ds(pl.multiple_of(HALF * (1 - core), HALF), HALF)
    gate_h, up_h, down_h = gate_hbm.at[0], up_hbm.at[0], down_hbm.at[0]
    loads = [
        pltpu.make_async_copy(k_hbm, k_s, lsem.at[0]),
        pltpu.make_async_copy(q_hbm, q_s, lsem.at[1]),
        pltpu.make_async_copy(v_hbm, v_s, lsem.at[2]),
        pltpu.make_async_copy(hin_hbm.at[:, half_cols], h_s.at[core], lsem.at[3]),
        pltpu.make_async_copy(wout_hbm, w_s.at[core], lsem.at[4]),
        pltpu.make_async_copy(gate_h, gate_s.at[core], lsem.at[5]),
        pltpu.make_async_copy(up_h, up_s.at[core], lsem.at[6]),
        pltpu.make_async_copy(down_h, down_s.at[core], lsem.at[7]),
        pltpu.make_async_copy(ids_hbm, ids_ref, lsem.at[8]),
        pltpu.make_async_copy(rw_hbm, rw_ref, lsem.at[9]),
        pltpu.make_async_copy(gain_hbm, gain_ref, lsem.at[10]),
    ]
    for load in loads:
        load.start()

    loads[0].wait()
    loads[1].wait()
    loads[2].wait()
    keys = k_s[...]
    vals = jnp.concatenate([v_s[...], jnp.ones((BLK, HD), BF16)], axis=1)
    diag = iota((PAIRS, HD), 0) == iota((PAIRS, HD), 1)
    stat_row = iota((16, HD), 0)

    def stats_block(pk, tt):
        pk0 = pk.astype(BF16).astype(F32)
        pk1 = (pk - pk0).astype(BF16).astype(F32)
        tt0 = tt.astype(BF16).astype(F32)
        stats = jnp.where(stat_row == 0, pk0, 0.0)
        for at, term in ((1, pk1), (2, pk - pk0 - pk1), (3, tt0), (4, tt - tt0)):
            stats = jnp.where(stat_row == at, term, stats)
        return stats.astype(BF16)

    def stats_of(block):
        stats = block[PAIRS:, :].astype(F32)
        return stats[0:1] + stats[1:2] + stats[2:3], stats[3:4] + stats[4:5]

    def as_column(row):
        return jnp.sum(jnp.where(diag, row, 0.0), axis=1, keepdims=True)

    def attend(half, into, start):
        first_limit = CONTEXT - Q - BLK * c
        rows, limits = [], []
        for i in range(start, start + GROUP):
            first = HALF * half + ROWS * owner(i)
            at = pl.ds(pl.multiple_of(first, ROWS), ROWS)
            for h in range(HEADS):
                rows.append(q_s[at, HD * h : HD * (h + 1)])
                limits.append(iota((ROWS, 1), 0) + (first_limit + first))
        qg = jnp.concatenate(rows, axis=0)
        limit = jnp.concatenate(limits, axis=0)
        scores = dot(qg, keys, ((1,), (1,))) * (math.log2(math.e) / math.sqrt(HD))
        scores = jnp.where(iota(scores.shape, 1) <= limit, scores, -1e30)
        peak = jnp.max(scores, axis=1, keepdims=True)
        both = dot(jnp.exp2(scores - peak).astype(BF16), vals)
        total = both[:, HD:]
        numer = (both[:, :HD] / total).astype(BF16)
        peaks = jnp.broadcast_to(peak, total.shape)
        for g in range(GROUP):
            part = slice(PAIRS * g, PAIRS * (g + 1))
            pk = jnp.sum(jnp.where(diag, peaks[part], 0.0), axis=0, keepdims=True)
            tt = jnp.sum(jnp.where(diag, total[part], 0.0), axis=0, keepdims=True)
            into[start + g, :PAIRS, :] = numer[part]
            into[start + g, PAIRS:, :] = stats_block(pk, tt)

    for start in range(0, CHIPS, GROUP):
        attend(1 - core, sib_s, start)
    for start in range(0, CHIPS, GROUP):
        attend(core, part_o, start)

    pl.semaphore_wait(barrier, 1 + (CHIPS - 1) + (EN - 1))

    for g in range(CHIPS // GROUP):
        some = pl.ds(GROUP * g, GROUP)
        push(sib_s.at[some], sibr_s.at[some], ksem.at[g], krsem.at[g], ctx=sib)
    push(hin_hbm.at[:, sib_cols], h_s.at[core], ssem.at[2], rsem.at[2], ctx=sib)
    push(wout_hbm, w_s.at[core], ssem.at[3], rsem.at[3], ctx=sib)
    push(gate_h, gate_s.at[core], ssem.at[4], rsem.at[4], ctx=sib)
    push(up_h, up_s.at[core], ssem.at[5], rsem.at[5], ctx=sib)
    push(down_h, down_s.at[core], ssem.at[6], rsem.at[6], ctx=sib)

    def merge(blocks):
        stats = [stats_of(block) for block in blocks]
        top = functools.reduce(jnp.maximum, [pk for pk, _ in stats])
        factors = [jnp.exp2(pk - top) * tt for pk, tt in stats]
        whole = sum(factors[1:], factors[0])
        inverse = 1.0 / jnp.maximum(whole, 1e-30)
        terms = [as_column(f * inverse) * block[:PAIRS, :].astype(F32) for f, block in zip(factors, blocks)]
        return sum(terms[1:], terms[0]).astype(BF16), top, whole

    def write(into, merged):
        numer, top, whole = merged
        into[:PAIRS, :] = numer
        into[PAIRS:, :] = stats_block(top, whole)

    def sibling_arrived(i):
        if i % GROUP == 0:
            arrived(sibr_s.at[pl.ds(i, GROUP)], krsem.at[i // GROUP])

    for i in range(ZN):
        sibling_arrived(i)
        write(num_s.at[i], merge([part_o.at[i], sibr_s.at[i]]))
        push(num_s.at[i], yin_s.at[i], vsem.at[i], vrsem.at[i], ctx=ypeer)
    for i in range(ZN):
        sibling_arrived(ZN + i)
        arrived(yin_s.at[i], vrsem.at[i])
        merged = merge([part_o.at[ZN + i], sibr_s.at[ZN + i], yin_s.at[i]])
        if AWAY[i]:
            write(num_s.at[ZN + i], merged)
            push(num_s.at[ZN + i], got_s.at[z], asem.at[i], arsem.at[z], ctx=at_chip(AWAY[i], y))
        else:
            write(own_s, merged)

    loads[8].wait()
    loads[9].wait()
    ids = ids_ref[...]
    owned = jnp.where((ids[0:1] == e) | (ids[1:2] == e), 1.0, 0.0)
    w_row = jnp.where(ids[0:1] == e, rw_ref[0:1, :], 0.0) + jnp.where(ids[1:2] == e, rw_ref[1:2, :], 0.0)
    before = jnp.where(iota((Q, Q), 0) < iota((Q, Q), 1), 1.0, 0.0).astype(BF16)
    rank = dot(jnp.broadcast_to(owned, (16, Q)).astype(BF16), before)[0:1]
    place = jnp.where(owned > 0.5, rank, -1.0)
    place_col = jnp.transpose(jnp.broadcast_to(place, (HD, Q)))
    for part in range(2):
        lane = (iota((Q, SH), 1) + SH * part).astype(F32)
        tok_s[:, SH * part : SH * (part + 1)] = jnp.where(place_col == lane, 1.0, 0.0).astype(BF16)
    slot_own = (iota((SH, Q), 0) + SH * core).astype(F32)
    w_slot = jnp.sum(jnp.where(place == slot_own, w_row, 0.0), axis=1, keepdims=True)

    blocks = [own_s]
    for d in AWAY[:-1]:
        blocks.append(got_s.at[near(d)])
        arrived(blocks[-1], arsem.at[near(d)])
    att_s[chip] = merge(blocks)[0]
    for d in FAR[:-1]:
        push(att_s.at[chip], att_s.at[chip], bsem.at[d], brsem.at[chip], ctx=2 * ((chip + d) % CHIPS) + core)
    for d in range(1, CHIPS):
        source = (chip + d) % CHIPS
        arrived(att_s.at[source], brsem.at[source])

    attended = jnp.concatenate(
        [att_s[:, ROWS * h : ROWS * (h + 1), :].reshape(HALF, HD) for h in range(HEADS)], axis=1
    )
    loads[4].wait()
    arrived(w_s.at[1 - core], rsem.at[3])
    projected = dot(attended, w_s[...].reshape(WIDE, HEADS * HD), ((1,), (1,)))
    own_p[...] = projected
    ps_s[...] = projected.astype(BF16).reshape(EN, TOKB, WIDE)
    for d in range(1, EN):
        to = (e + d) % EN
        push(ps_s.at[to], pr_s.at[e], psem.at[d], prsem.at[e], ex=to)
    loads[3].wait()
    arrived(h_s.at[1 - core], rsem.at[2])
    my_tokens = jnp.where(iota((TOKB, HALF), 1) == iota((TOKB, HALF), 0) + TOKB * e, 1.0, 0.0).astype(BF16)
    before_attention = dot(my_tokens, h_s[...].reshape(WIDE, HALF), ((1,), (1,)))
    stream = own_p[pl.ds(pl.multiple_of(TOKB * e, TOKB), TOKB), :]
    for d in range(1, EN):
        source = (e + d) % EN
        arrived(pr_s.at[source], prsem.at[source])
        stream = stream + pr_s[source].astype(F32)
    stream = stream + before_attention
    st_s[e] = stream.astype(BF16)
    for d in range(1, EN):
        to = (e + d) % EN
        push(st_s.at[e], st_s.at[e], gsem.at[d], grsem.at[e], ex=to)
    for d in range(1, EN):
        source = (e + d) % EN
        arrived(st_s.at[source], grsem.at[source])

    rows = st_s[...].reshape(HALF, WIDE)

    def slots_of(part):
        token = iota((SH, HALF), 1) + HALF * core
        pick = iota((SH, HALF), 0) + SH * part
        here = jnp.where(core == 0, place[:, :HALF], place[:, HALF:])
        hot = jnp.where(here == pick.astype(F32), 1.0, 0.0).astype(BF16)
        return dot(hot, rows)

    xs_s[...] = slots_of(1 - core).astype(BF16)
    push(xs_s, xr_s, ssem.at[7], rsem.at[7], ctx=sib)
    resid = st_s[pl.ds(2 * (e % 4), 2)].reshape(OUTR, WIDE)
    take_own = jnp.where(iota((WIDE, 256), 0) == iota((WIDE, 256), 1) + COLS * core, 1.0, 0.0)
    take_sib = jnp.where(iota((WIDE, 256), 0) == iota((WIDE, 256), 1) + COLS * (1 - core), 1.0, 0.0)
    valid = iota((WIDE, 256), 1) < COLS
    take_own = jnp.where(valid, take_own, 0.0).astype(BF16)
    take_sib = jnp.where(valid, take_sib, 0.0).astype(BF16)
    rs_s[...] = dot(resid, take_sib).astype(BF16)
    push(rs_s, rr_s, ssem.at[8], rsem.at[8], ctx=sib)
    resid_own = dot(resid, take_own)
    mine = slots_of(core)
    arrived(xr_s, rsem.at[7])
    x_s[z, y] = (mine + xr_s[...].astype(F32)).astype(BF16)

    PART = SQ // 2
    low_half = pl.ds(SQ, SQ)

    def x_low(d, yy):
        return x_s.at[near(d), yy, low_half, :]

    def x_top(d, part):
        return x_s.at[near(d), :, pl.ds(PART * part, PART), :]

    def x_one(d, yy, part):
        return x_s.at[near(d), yy, pl.ds(PART * part, PART), :]

    FR, FL, TR, TL, LR, LL = (0, 2), (4, 6), (10, 13), (16, 18), 20, 23

    def first_hops(part, base, d):
        mine = x_one(0, y, part)
        for yy in (y, 1 - y):
            push(mine, mine, xsem.at[base[part] + yy], xrsem.at[base[part] + y], ctx=at_chip(d, yy))

    push(x_low(0, y), x_low(0, y), xsem.at[LL], xrsem.at[LL], ctx=left)
    first_hops(0, FR, 1)
    first_hops(1, FR, 1)
    first_hops(0, FL, -1)
    first_hops(1, FL, -1)
    push(x_low(0, y), x_low(0, y), xsem.at[LR], xrsem.at[LR], ctx=right)
    push(x_low(0, y), x_low(0, y), tsem.at[0], trsem.at[z], ctx=ypeer)
    for part in range(2):
        push(x_one(0, y, part), x_one(0, y, part), xsem.at[8 + part], xrsem.at[8 + part], ctx=ypeer)
    drain(13)

    loads[5].wait()
    loads[6].wait()
    loads[10].wait()
    arrived(gate_s.at[1 - core], rsem.at[4])
    arrived(up_s.at[1 - core], rsem.at[5])
    acc_s[...] = jnp.zeros_like(acc_s)
    sq_s[...] = jnp.zeros_like(sq_s)

    def project(d):
        zz = near(d)
        for yy in range(2):
            at = pl.ds(pl.multiple_of(WIDE * (2 * zz + yy), WIDE), WIDE)
            block = x_s[zz, yy].astype(F32)
            square = block * block
            sq_s[...] += square[:, :128] + square[:, 128:256] + square[:, 256:]
            scaled = (block * gain_ref[:, at]).astype(BF16)
            for kk in range(2):
                acc_s[0, kk] += dot(scaled, gate_s[kk, at, :])
                acc_s[1, kk] += dot(scaled, up_s[kk, at, :])

    def low_arrived(d):
        arrived(x_low(d, 1 - y), trsem.at[near(d)])

    def top_on(d, s, part, first, base, last, to):
        if s == 1:
            for yy in range(2):
                arrived(x_one(d, yy, part), xrsem.at[first[part] + yy])
        else:
            arrived(x_top(d, part), xrsem.at[base[part] + s - 2])
        if s < last:
            push(x_top(d, part), x_top(d, part), xsem.at[base[part] + s - 1], xrsem.at[base[part] + s - 1], ctx=to)

    def low_on(d, s, base, last, to):
        block = x_low(d, y)
        arrived(block, xrsem.at[base + s - 1])
        if s < last:
            push(block, block, xsem.at[base + s], xrsem.at[base + s], ctx=to)
        if s <= 3:
            push(block, block, tsem.at[d % ZN], trsem.at[near(d)], ctx=ypeer)
        if d == 3:
            push(block, block, tsem.at[4], trsem.at[near(d)], ctx=at_chip(-1, 1 - y))

    for s in range(1, 5):
        low_on(s, s, LL, 4, left)
        for part in range(2):
            top_on(-s, s, part, FR, TR, 4, right)
            if s <= 3:
                top_on(s, s, part, FL, TL, 3, left)
        if s <= 3:
            low_on(-s, s, LR, 3, right)
        if s == 1:
            for part in range(2):
                arrived(x_one(0, 1 - y, part), xrsem.at[8 + part])
            low_arrived(0)
            project(0)
        else:
            low_arrived(s - 1)
            project(s - 1)
            low_arrived(1 - s)
            project(1 - s)
    low_arrived(4)
    project(4)

    inverse_rms = lax.rsqrt(jnp.sum(sq_s[...], axis=1, keepdims=True) / D + 1e-5)
    hidden = []
    for kk in range(2):
        gate_val = acc_s[0, kk] * inverse_rms
        up_val = acc_s[1, kk] * inverse_rms
        hidden.append((gate_val / (1.0 + jnp.exp(-gate_val)) * up_val).astype(BF16))
    loads[7].wait()
    arrived(down_s.at[1 - core], rsem.at[6])

    def expand(d):
        zz = near(d)
        for yy in range(2):
            at = pl.ds(pl.multiple_of(WIDE * (2 * zz + yy), WIDE), WIDE)
            part_s[zz, yy] = dot(hidden[0], down_s[0, :, at]) + dot(hidden[1], down_s[1, :, at])
        if d == 0:
            f1s[...] = part_s[zz, 1 - y, :SQ, :].astype(BF16)
            push(f1s, f1r, ssem.at[9], rsem.at[9], ctx=ypeer)
        if d != 4:
            ys_s[zz] = part_s[zz, 1 - y, SQ:, :].astype(BF16)
            push(ys_s.at[zz], yr_s.at[zz], ysem.at[d % ZN], yrsem.at[zz], ctx=ypeer)

    def top_step(d, s, last, part, out_s, in_s, base, step):
        value = part_s[near(d), :, PART * part : PART * (part + 1), :]
        if s:
            arrived(in_s.at[s - 1, part], ersem.at[base + s - 1])
            value = value + in_s[s - 1, part].astype(F32)
        out_s[s, part] = value.astype(BF16)
        if s < last:
            push(out_s.at[s, part], in_s.at[s, part], esem.at[base + s], ersem.at[base + s], ctx=at_chip(step, y))
        else:
            for yy in (y, 1 - y):
                push(
                    out_s.at[s, part, yy], in_s.at[s, part, y],
                    esem.at[base + s + yy], ersem.at[base + s + y], ctx=at_chip(step, yy),
                )

    def top_right(s):
        for part in range(2):
            top_step(4 - s, s, 3, part, h1rs, h1rr, 5 * part, 1)

    def top_left(s):
        for part in range(2):
            top_step(s - 3, s, 2, part, h1ls, h1lr, 10 + 4 * part, -1)

    def low_value(d):
        arrived(yr_s.at[near(d)], yrsem.at[near(d)])
        return part_s[near(d), y, SQ:, :] + yr_s[near(d)].astype(F32)

    def low_right(s):
        value = low_value(3 - s)
        if s:
            arrived(h2rr.at[s - 1], ersem.at[17 + s])
            value = value + h2rr[s - 1].astype(F32)
        h2rs[s] = value.astype(BF16)
        push(h2rs.at[s], h2rr.at[s], esem.at[18 + s], ersem.at[18 + s], ctx=right)

    def low_left(s):
        if s == 0:
            h2fs[...] = part_s[near(4), :, SQ:, :].astype(BF16)
            for yy in (y, 1 - y):
                push(h2fs.at[yy], h2fr.at[y], esem.at[21 + yy], ersem.at[21 + y], ctx=at_chip(-1, yy))
            return
        value = low_value(s - 4)
        if s == 1:
            for yy in range(2):
                arrived(h2fr.at[yy], ersem.at[21 + yy])
                value = value + h2fr[yy].astype(F32)
        else:
            arrived(h2lr.at[s - 1], ersem.at[21 + s])
            value = value + h2lr[s - 1].astype(F32)
        h2ls[s] = value.astype(BF16)
        push(h2ls.at[s], h2lr.at[s], esem.at[22 + s], ersem.at[22 + s], ctx=left)

    expand(4)
    top_right(0)
    low_left(0)
    expand(-3)
    top_left(0)
    for d in (3, -2, 2, -1, 1, 0):
        expand(d)
    for s in range(1, 4):
        top_right(s)
        low_left(s)
        if s < 3:
            top_left(s)
        low_right(s - 1)
    drain(8)
    arrived(f1r, rsem.at[9])
    top_sum = part_s[z, y, :SQ, :] + f1r[...].astype(F32)
    ends = []
    for part in range(2):
        end = top_sum[PART * part : PART * (part + 1)]
        for yy in range(2):
            arrived(h1rr.at[3, part, yy], ersem.at[5 * part + 3 + yy])
            arrived(h1lr.at[2, part, yy], ersem.at[10 + 4 * part + 2 + yy])
            end = end + (h1rr[3, part, yy].astype(F32) + h1lr[2, part, yy].astype(F32))
        ends.append(end)
    low_sum = low_value(0)
    arrived(h2rr.at[2], ersem.at[20])
    arrived(h2lr.at[3], ersem.at[25])
    low_sum = low_sum + (h2rr[2].astype(F32) + h2lr[3].astype(F32))
    summed = (jnp.concatenate([*ends, low_sum], axis=0) * w_slot).astype(BF16)

    os_s[...] = dot(summed, take_sib).astype(BF16)
    push(os_s, or_s, ssem.at[10], rsem.at[10], ctx=sib)
    own_cols = dot(summed, take_own).astype(BF16)
    arrived(or_s, rsem.at[10])
    o_s[core] = own_cols
    o_s[1 - core] = or_s[...]
    slots = o_s[...].reshape(SLOTS, 256)
    town_s[...] = dot(tok_s[...], slots).reshape(EN, OUTR, 256)
    ts_s[...] = town_s[...].astype(BF16)
    for d in range(1, EN):
        to = (e + d) % EN
        push(ts_s.at[to], tr_s.at[e], psem.at[EN + d], prsem.at[EN + e], ex=to)
    arrived(rr_s, rsem.at[8])
    mixed = town_s[e] + jnp.where(core == e // 4, resid_own, rr_s[...].astype(F32))
    for d in range(1, EN):
        source = (e + d) % EN
        arrived(tr_s.at[source], prsem.at[EN + source])
        mixed = mixed + tr_s[source].astype(F32)
    out_ref[...] = mixed[:, :COLS].astype(BF16)
    drain()


def local(hidden_in, queries, keys, values, out_weight, norm_gain, expert_gate, expert_up, expert_down, expert_ids, route_weights):
    vmem = pl.BlockSpec(memory_space=pltpu.VMEM)
    anywhere = pl.BlockSpec(memory_space=pl.ANY)
    dma = pltpu.SemaphoreType.DMA

    def buf(*shape, dtype=BF16):
        return pltpu.VMEM(shape, dtype)

    scratch = [
        buf(2, Q, dtype=jnp.int32), buf(2, Q, dtype=F32), buf(1, D, dtype=F32),
        buf(Q, HEADS * HD), buf(BLK, HD), buf(BLK, HD), buf(2, COLS, HALF),
        buf(2, COLS, HEADS * HD),
        buf(2, D, FF), buf(2, D, FF), buf(2, FF, D),
        buf(CHIPS, MSG, HD), buf(CHIPS, MSG, HD), buf(CHIPS, MSG, HD),
        buf(ZN, MSG, HD), buf(CHIPS, MSG, HD), buf(ZN, MSG, HD), buf(MSG, HD), buf(CHIPS, PAIRS, HD),
        buf(EN, TOKB, WIDE), buf(EN, TOKB, WIDE), buf(HALF, WIDE, dtype=F32), buf(EN, TOKB, WIDE),
        buf(SH, WIDE), buf(SH, WIDE), buf(ZN, 2, SH, WIDE),
        buf(2, 2, SH, FF, dtype=F32), buf(SH, 128, dtype=F32), buf(ZN, 2, SH, WIDE, dtype=F32),
        buf(ZN, SQ, WIDE), buf(ZN, SQ, WIDE),
        buf(4, 2, 2, SQ // 2, WIDE), buf(4, 2, 2, SQ // 2, WIDE), buf(3, 2, 2, SQ // 2, WIDE), buf(3, 2, 2, SQ // 2, WIDE),
        buf(3, SQ, WIDE), buf(3, SQ, WIDE), buf(4, SQ, WIDE), buf(4, SQ, WIDE),
        buf(2, SQ, WIDE), buf(2, SQ, WIDE), buf(SQ, WIDE), buf(SQ, WIDE),
        buf(2, SH, 256), buf(SH, 256), buf(SH, 256), buf(OUTR, 256), buf(OUTR, 256),
        buf(EN, OUTR, 256), buf(EN, OUTR, 256), buf(EN, OUTR, 256, dtype=F32), buf(Q, SLOTS),
        dma((11,)), dma((11,)), dma((11,)),
        dma((CHIPS,)), dma((CHIPS,)), dma((CHIPS,)), dma((CHIPS,)),
        dma((2 * EN,)), dma((2 * EN,)), dma((EN,)), dma((EN,)), dma((ZN,)), dma((ZN,)),
        dma((ZN,)), dma((ZN,)), dma((27,)), dma((27,)), dma((26,)), dma((26,)), dma((4,)), dma((4,)),
        dma((ZN,)), dma((ZN,)),
    ]
    return pl.pallas_call(
        layer_kernel,
        out_shape=jax.ShapeDtypeStruct((OUTR, COLS), BF16),
        in_specs=[anywhere] * 11,
        out_specs=vmem,
        scratch_shapes=scratch,
        compiler_params=pltpu.CompilerParams(
            collective_id=0, has_side_effects=True, vmem_limit_bytes=56 * 1024 * 1024
        ),
        cost_estimate=pl.CostEstimate(flops=3 * 10**9, bytes_accessed=12 * 10**6, transcendentals=2 * 10**6),
    )(
        expert_ids.T, route_weights.T, norm_gain.reshape(1, D), queries, keys, values, hidden_in.T,
        out_weight.T, expert_gate, expert_up, expert_down,
    )


def solution(mesh):
    placed = (
        P(None, "ctx"),
        P(None, "exp"),
        P("ctx", "exp"),
        P("ctx", "exp"),
        P("exp", "ctx"),
        P(),
        P("exp", None, "ctx"),
        P("exp", None, "ctx"),
        P("exp", "ctx", None),
        P(),
        P(),
    )
    return jax.shard_map(
        local, mesh=mesh, in_specs=placed, out_specs=P("exp", "ctx"), check_vma=False
    )
```

```python
import functools
import math

import jax
import jax.numpy as jnp
from jax import lax
from jax.experimental import pallas as pl
from jax.experimental.pallas import tpu as pltpu
from jax.sharding import PartitionSpec as P

F32 = jnp.float32
BF16 = jnp.bfloat16
MESH = pl.DeviceIdType.MESH

HD = 128
D = 6144
Q = 512
CONTEXT = 16384
CHIPS = 16
ZN = 8
EN = 8
HEADS = 6
HALF = Q // 2
ROWS = HALF // CHIPS
PAIRS = ROWS * HEADS
BLK = 512
WIDE = 384
COLS = 192
SLOTS = 256
SH = SLOTS // 2
SQ = SH // 2
TOKB = HALF // EN
OUTR = Q // EN
FF = 256
PACK = OUTR + OUTR // 2
MSG = PAIRS + 16
GROUP = 4
AWAY = (4, -3, 3, -2, 2, -1, 1, 0)


def dot(a, b, dims=((1,), (0,))):
    return lax.dot_general(a, b, (dims, ((), ())), preferred_element_type=F32)


def iota(shape, dim):
    return lax.broadcasted_iota(jnp.int32, shape, dim)


def layer_kernel(
    ids_hbm, rw_hbm, gain_hbm, q_hbm, k_hbm, v_hbm, hin_hbm, wout_hbm, gate_hbm, up_hbm, down_hbm,
    out_ref,
    ids_ref, rw_ref, gain_ref, q_s, k_s, v_s, h_s, w_s, gate_s, up_s, down_s,
    sib_s, sibr_s, part_o, yin_s, num_s, got_s, own_s, att_s, ps_s, pr_s, own_p, st_s,
    xs_s, xr_s, x_s, acc_s, sq_s, part_s, ys_s, yr_s,
    h1rs, h1rr, h1ls, h1lr, h2rs, h2rr, h2ls, h2lr, h2fs, h2fr, f1s, f1r,
    o_s, os_s, or_s, rs_s, rr_s, ts_s, tr_s, town_s, tok_s,
    lsem, ssem, rsem, tosem, krsem, vrsem, arsem, brsem, prsem, trsem, yrsem, xrsem, ersem,
):
    c = lax.axis_index("ctx")
    e = lax.axis_index("exp")
    core = c % 2
    chip = c // 2
    y = chip % 2
    z = chip // 2
    sib = c + 1 - 2 * core
    ypeer = c + 2 - 4 * y
    zp = [(z + d) % ZN for d in range(ZN)]

    def near(d):
        return zp[d % ZN]

    def at_chip(d, yy):
        return near(d) * 4 + yy * 2 + core

    right, left = at_chip(1, y), at_chip(-1, y)

    def owner(i):
        return near(AWAY[i % ZN]) * 2 + (1 - y if i < ZN else y)

    def remote(src, dst, send, recv, ctx=None, ex=None):
        return pltpu.make_async_remote_copy(
            src_ref=src, dst_ref=dst, send_sem=send, recv_sem=recv,
            device_id=(c if ctx is None else ctx, e if ex is None else ex),
            device_id_type=MESH,
        )

    def arrived(ref, sem):
        pltpu.make_async_copy(ref, ref, sem).wait()

    sent = []

    def push(*args, **kw):
        copy = remote(*args, **kw)
        copy.start()
        sent.append(copy)

    (TO_SIB, TO_Y, TO_Z, TO_CHIPS, TO_EXP, TO_EXP_ALL, TO_LOW_Y, TO_FIRST, TO_PAIRS, TO_LOW, TO_SUM_Y,
     TO_TR, TO_TL, TO_LR, TO_LF, TO_LL, TO_TOK) = range(17)

    def send(src, dst, kind, recv, **kw):
        remote(src, dst, tosem.at[kind], recv, **kw).start()

    def left_here(ref, kind):
        remote(ref, ref, tosem.at[kind], tosem.at[kind], ctx=sib).wait_send()

    barrier = pltpu.get_barrier_semaphore()

    def greet(ctx, ex):
        pl.semaphore_signal(barrier, inc=1, device_id=(ctx, ex), device_id_type=MESH)

    greet(sib, e)
    for d in range(1, CHIPS):
        greet(2 * ((chip + d) % CHIPS) + core, e)
    for d in range(1, EN):
        greet(c, (e + d) % EN)

    half_cols = pl.ds(pl.multiple_of(HALF * core, HALF), HALF)
    sib_cols = pl.ds(pl.multiple_of(HALF * (1 - core), HALF), HALF)
    gate_h, up_h, down_h = gate_hbm.at[0], up_hbm.at[0], down_hbm.at[0]
    loads = [
        pltpu.make_async_copy(k_hbm, k_s, lsem.at[0]),
        pltpu.make_async_copy(q_hbm, q_s, lsem.at[1]),
        pltpu.make_async_copy(v_hbm, v_s, lsem.at[2]),
        pltpu.make_async_copy(hin_hbm.at[:, half_cols], h_s.at[core], lsem.at[3]),
        pltpu.make_async_copy(wout_hbm, w_s.at[core], lsem.at[4]),
        pltpu.make_async_copy(gate_h, gate_s.at[core], lsem.at[5]),
        pltpu.make_async_copy(up_h, up_s.at[core], lsem.at[6]),
        pltpu.make_async_copy(down_h, down_s.at[core], lsem.at[7]),
        pltpu.make_async_copy(ids_hbm, ids_ref, lsem.at[8]),
        pltpu.make_async_copy(rw_hbm, rw_ref, lsem.at[9]),
        pltpu.make_async_copy(gain_hbm, gain_ref, lsem.at[10]),
    ]
    for load in loads:
        load.start()

    loads[0].wait()
    loads[1].wait()
    loads[2].wait()
    keys = k_s[...]
    vals = jnp.concatenate([v_s[...], jnp.ones((BLK, HD), BF16)], axis=1)
    diag = iota((PAIRS, HD), 0) == iota((PAIRS, HD), 1)
    stat_row = iota((16, HD), 0)

    def stats_block(pk, tt):
        pk0 = pk.astype(BF16).astype(F32)
        pk1 = (pk - pk0).astype(BF16).astype(F32)
        tt0 = tt.astype(BF16).astype(F32)
        stats = jnp.where(stat_row == 0, pk0, 0.0)
        for at, term in ((1, pk1), (2, pk - pk0 - pk1), (3, tt0), (4, tt - tt0)):
            stats = jnp.where(stat_row == at, term, stats)
        return stats.astype(BF16)

    def stats_of(block):
        stats = block[PAIRS:, :].astype(F32)
        return stats[0:1] + stats[1:2] + stats[2:3], stats[3:4] + stats[4:5]

    def as_column(row):
        return jnp.sum(jnp.where(diag, row, 0.0), axis=1, keepdims=True)

    def attend(half, into, start):
        first_limit = CONTEXT - Q - BLK * c
        rows, limits = [], []
        for i in range(start, start + GROUP):
            first = HALF * half + ROWS * owner(i)
            at = pl.ds(pl.multiple_of(first, ROWS), ROWS)
            for h in range(HEADS):
                rows.append(q_s[at, HD * h : HD * (h + 1)])
                limits.append(iota((ROWS, 1), 0) + (first_limit + first))
        qg = jnp.concatenate(rows, axis=0)
        limit = jnp.concatenate(limits, axis=0)
        scores = dot(qg, keys, ((1,), (1,))) * (math.log2(math.e) / math.sqrt(HD))
        scores = jnp.where(iota(scores.shape, 1) <= limit, scores, -1e30)
        peak = jnp.max(scores, axis=1, keepdims=True)
        both = dot(jnp.exp2(scores - peak).astype(BF16), vals)
        total = both[:, HD:]
        numer = (both[:, :HD] / total).astype(BF16)
        peaks = jnp.broadcast_to(peak, total.shape)
        for g in range(GROUP):
            part = slice(PAIRS * g, PAIRS * (g + 1))
            pk = jnp.sum(jnp.where(diag, peaks[part], 0.0), axis=0, keepdims=True)
            tt = jnp.sum(jnp.where(diag, total[part], 0.0), axis=0, keepdims=True)
            into[start + g, :PAIRS, :] = numer[part]
            into[start + g, PAIRS:, :] = stats_block(pk, tt)

    for start in range(0, CHIPS, GROUP):
        attend(1 - core, sib_s, start)
    for start in range(0, CHIPS, GROUP):
        attend(core, part_o, start)

    pl.semaphore_wait(barrier, 1 + (CHIPS - 1) + (EN - 1))

    for g in range(CHIPS // GROUP):
        some = pl.ds(GROUP * g, GROUP)
        send(sib_s.at[some], sibr_s.at[some], TO_SIB, krsem.at[g], ctx=sib)
    push(hin_hbm.at[:, sib_cols], h_s.at[core], ssem.at[2], rsem.at[2], ctx=sib)
    push(wout_hbm, w_s.at[core], ssem.at[3], rsem.at[3], ctx=sib)
    push(gate_h, gate_s.at[core], ssem.at[4], rsem.at[4], ctx=sib)
    push(up_h, up_s.at[core], ssem.at[5], rsem.at[5], ctx=sib)
    push(down_h, down_s.at[core], ssem.at[6], rsem.at[6], ctx=sib)

    def merge(blocks):
        stats = [stats_of(block) for block in blocks]
        top = functools.reduce(jnp.maximum, [pk for pk, _ in stats])
        factors = [jnp.exp2(pk - top) * tt for pk, tt in stats]
        whole = sum(factors[1:], factors[0])
        inverse = 1.0 / jnp.maximum(whole, 1e-30)
        terms = [as_column(f * inverse) * block[:PAIRS, :].astype(F32) for f, block in zip(factors, blocks)]
        return sum(terms[1:], terms[0]).astype(BF16), top, whole

    def write(into, merged):
        numer, top, whole = merged
        into[:PAIRS, :] = numer
        into[PAIRS:, :] = stats_block(top, whole)

    def sibling_arrived(i):
        if i % GROUP == 0:
            arrived(sibr_s.at[pl.ds(i, GROUP)], krsem.at[i // GROUP])

    for i in range(ZN):
        sibling_arrived(i)
        write(num_s.at[i], merge([part_o.at[i], sibr_s.at[i]]))
        send(num_s.at[i], yin_s.at[i], TO_Y, vrsem.at[i], ctx=ypeer)
    for i in range(ZN):
        sibling_arrived(ZN + i)
        arrived(yin_s.at[i], vrsem.at[i])
        merged = merge([part_o.at[ZN + i], sibr_s.at[ZN + i], yin_s.at[i]])
        if AWAY[i]:
            write(num_s.at[ZN + i], merged)
            send(num_s.at[ZN + i], got_s.at[z], TO_Z, arsem.at[0], ctx=at_chip(AWAY[i], y))
        else:
            write(own_s, merged)

    loads[8].wait()
    loads[9].wait()
    ids = ids_ref[...]
    owned = jnp.where((ids[0:1] == e) | (ids[1:2] == e), 1.0, 0.0)
    w_row = jnp.where(ids[0:1] == e, rw_ref[0:1, :], 0.0) + jnp.where(ids[1:2] == e, rw_ref[1:2, :], 0.0)
    before = jnp.where(iota((Q, Q), 0) < iota((Q, Q), 1), 1.0, 0.0).astype(BF16)
    rank = dot(jnp.broadcast_to(owned, (16, Q)).astype(BF16), before)[0:1]
    place = jnp.where(owned > 0.5, rank, -1.0)
    place_col = jnp.transpose(jnp.broadcast_to(place, (HD, Q)))
    for part in range(2):
        lane = (iota((Q, SH), 1) + SH * part).astype(F32)
        tok_s[:, SH * part : SH * (part + 1)] = jnp.where(place_col == lane, 1.0, 0.0).astype(BF16)
    slot_own = (iota((SH, Q), 0) + SH * core).astype(F32)
    w_slot = jnp.sum(jnp.where(place == slot_own, w_row, 0.0), axis=1, keepdims=True)

    arrived(got_s.at[pl.ds(0, ZN - 1)], arsem.at[0])
    att_s[chip] = merge([own_s] + [got_s.at[near(d)] for d in AWAY[:-1]])[0]
    for d in AWAY:
        for yy in (y, 1 - y):
            if d or yy is not y:
                send(att_s.at[chip], att_s.at[chip], TO_CHIPS, brsem.at[chip], ctx=at_chip(d, yy))

    loads[4].wait()
    arrived(w_s.at[1 - core], rsem.at[3])
    weight = w_s[...].reshape(WIDE, HEADS * HD)
    for d in (0, *AWAY[:-1]):
        to = near(d)
        for source in (2 * to, 2 * to + 1) if d else (2 * z + 1 - y,):
            arrived(att_s.at[source], brsem.at[source])
        pair = att_s[pl.ds(2 * to, 2)]
        attended = jnp.concatenate(
            [pair[:, ROWS * h : ROWS * (h + 1), :].reshape(TOKB, HD) for h in range(HEADS)], axis=1
        )
        projected = dot(attended, weight, ((1,), (1,)))
        ps_s[to] = projected.astype(BF16)

        @pl.when(to == e)
        def _(projected=projected):
            own_p[...] = projected

        @pl.when(to != e)
        def _(to=to):
            send(ps_s.at[to], pr_s.at[e], TO_EXP, prsem.at[0], ex=to)

    loads[3].wait()
    arrived(h_s.at[1 - core], rsem.at[2])
    my_tokens = jnp.where(iota((TOKB, HALF), 1) == iota((TOKB, HALF), 0) + TOKB * e, 1.0, 0.0).astype(BF16)
    before_attention = dot(my_tokens, h_s[...].reshape(WIDE, HALF), ((1,), (1,)))
    stream = own_p[...]
    arrived(pr_s.at[pl.ds(0, EN - 1)], prsem.at[0])
    for d in range(1, EN):
        source = (e + d) % EN
        stream = stream + pr_s[source].astype(F32)
    stream = stream + before_attention
    st_s[e] = stream.astype(BF16)
    for d in range(1, EN):
        to = (e + d) % EN
        send(st_s.at[e], st_s.at[e], TO_EXP_ALL, prsem.at[1], ex=to)
    arrived(st_s.at[pl.ds(0, EN - 1)], prsem.at[1])

    rows = st_s[...].reshape(HALF, WIDE)

    def slots_of(part):
        token = iota((SH, HALF), 1) + HALF * core
        pick = iota((SH, HALF), 0) + SH * part
        here = jnp.where(core == 0, place[:, :HALF], place[:, HALF:])
        hot = jnp.where(here == pick.astype(F32), 1.0, 0.0).astype(BF16)
        return dot(hot, rows)

    xs_s[...] = slots_of(1 - core).astype(BF16)
    push(xs_s, xr_s, ssem.at[7], rsem.at[7], ctx=sib)
    resid = st_s[pl.ds(2 * (e % 4), 2)].reshape(OUTR, WIDE)
    take_own = jnp.where(iota((WIDE, 256), 0) == iota((WIDE, 256), 1) + COLS * core, 1.0, 0.0)
    take_sib = jnp.where(iota((WIDE, 256), 0) == iota((WIDE, 256), 1) + COLS * (1 - core), 1.0, 0.0)
    valid = iota((WIDE, 256), 1) < COLS
    take_own = jnp.where(valid, take_own, 0.0).astype(BF16)
    take_sib = jnp.where(valid, take_sib, 0.0).astype(BF16)
    rs_s[...] = dot(resid, take_sib).astype(BF16)
    push(rs_s, rr_s, ssem.at[8], rsem.at[8], ctx=sib)
    resid_own = dot(resid, take_own)
    mine = slots_of(core)
    arrived(xr_s, rsem.at[7])
    x_s[z, y] = (mine + xr_s[...].astype(F32)).astype(BF16)

    PART = SQ // 2
    low_half = pl.ds(SQ, SQ)

    def x_low(d, yy):
        return x_s.at[near(d), yy, low_half, :]

    def x_top(d, part):
        return x_s.at[near(d), :, pl.ds(PART * part, PART), :]

    def x_one(d, yy, part):
        return x_s.at[near(d), yy, pl.ds(PART * part, PART), :]

    FR, FL, OY, TR, TL, LR, LL = 0, 2, 4, (6, 9), (12, 14), 16, 19

    def same(block, kind, recv, to):
        send(block, block, kind, recv, ctx=to)

    def first_hops(part, base, d):
        for yy in (y, 1 - y):
            same(x_one(0, y, part), TO_FIRST, xrsem.at[base + part], at_chip(d, yy))

    same(x_low(0, y), TO_LOW, xrsem.at[LL], left)
    first_hops(0, FR, 1)
    first_hops(1, FR, 1)
    first_hops(0, FL, -1)
    first_hops(1, FL, -1)
    same(x_low(0, y), TO_LOW, xrsem.at[LR], right)
    same(x_low(0, y), TO_LOW_Y, trsem.at[z], ypeer)
    for part in range(2):
        same(x_one(0, y, part), TO_FIRST, xrsem.at[OY + part], ypeer)

    loads[5].wait()
    loads[6].wait()
    loads[10].wait()
    arrived(gate_s.at[1 - core], rsem.at[4])
    arrived(up_s.at[1 - core], rsem.at[5])
    acc_s[...] = jnp.zeros_like(acc_s)
    sq_s[...] = jnp.zeros_like(sq_s)

    def project(d):
        zz = near(d)
        for yy in range(2):
            at = pl.ds(pl.multiple_of(WIDE * (2 * zz + yy), WIDE), WIDE)
            block = x_s[zz, yy].astype(F32)
            square = block * block
            sq_s[...] += square[:, :128] + square[:, 128:256] + square[:, 256:]
            scaled = (block * gain_ref[:, at]).astype(BF16)
            for kk in range(2):
                acc_s[0, kk] += dot(scaled, gate_s[kk, at, :])
                acc_s[1, kk] += dot(scaled, up_s[kk, at, :])

    def low_arrived(d):
        arrived(x_low(d, 1 - y), trsem.at[near(d)])

    def top_on(d, s, part, first, base, last, to):
        arrived(x_top(d, part), xrsem.at[first + part if s == 1 else base[part] + s - 2])
        if s < last:
            same(x_top(d, part), TO_PAIRS, xrsem.at[base[part] + s - 1], to)

    def low_on(d, s, base, last, to):
        block = x_low(d, y)
        arrived(block, xrsem.at[base + s - 1])
        if s < last:
            same(block, TO_LOW, xrsem.at[base + s], to)
        if s <= 3:
            same(block, TO_LOW_Y, trsem.at[near(d)], ypeer)
        if d == 3:
            same(block, TO_LOW_Y, trsem.at[near(d)], at_chip(-1, 1 - y))

    for s in range(1, 5):
        low_on(s, s, LL, 4, left)
        for part in range(2):
            top_on(-s, s, part, FR, TR, 4, right)
            if s <= 3:
                top_on(s, s, part, FL, TL, 3, left)
        if s <= 3:
            low_on(-s, s, LR, 3, right)
        if s == 1:
            for part in range(2):
                arrived(x_one(0, 1 - y, part), xrsem.at[OY + part])
            low_arrived(0)
            project(0)
        else:
            low_arrived(s - 1)
            project(s - 1)
            low_arrived(1 - s)
            project(1 - s)
    low_arrived(4)
    project(4)

    inverse_rms = lax.rsqrt(jnp.sum(sq_s[...], axis=1, keepdims=True) / D + 1e-5)
    hidden = []
    for kk in range(2):
        gate_val = acc_s[0, kk] * inverse_rms
        up_val = acc_s[1, kk] * inverse_rms
        hidden.append((gate_val / (1.0 + jnp.exp(-gate_val)) * up_val).astype(BF16))
    loads[7].wait()
    arrived(down_s.at[1 - core], rsem.at[6])

    def expand(d):
        zz = near(d)
        for yy in range(2):
            at = pl.ds(pl.multiple_of(WIDE * (2 * zz + yy), WIDE), WIDE)
            part_s[zz, yy] = dot(hidden[0], down_s[0, :, at]) + dot(hidden[1], down_s[1, :, at])
        if d == 0:
            f1s[...] = part_s[zz, 1 - y, :SQ, :].astype(BF16)
            push(f1s, f1r, ssem.at[9], rsem.at[9], ctx=ypeer)
        if d != 4:
            ys_s[zz] = part_s[zz, 1 - y, SQ:, :].astype(BF16)
            send(ys_s.at[zz], yr_s.at[zz], TO_SUM_Y, yrsem.at[zz], ctx=ypeer)

    def top_step(d, s, last, part, out_s, in_s, kind, base, step):
        value = part_s[near(d), :, PART * part : PART * (part + 1), :]
        if s:
            arrived(in_s.at[s - 1, part], ersem.at[base + s - 1])
            value = value + in_s[s - 1, part].astype(F32)
        out_s[s, part] = value.astype(BF16)
        if s < last:
            send(out_s.at[s, part], in_s.at[s, part], kind, ersem.at[base + s], ctx=at_chip(step, y))
        else:
            for yy in (y, 1 - y):
                send(out_s.at[s, part, yy], in_s.at[s, part, y], kind, ersem.at[base + s], ctx=at_chip(step, yy))

    def top_right(s):
        for part in range(2):
            top_step(4 - s, s, 3, part, h1rs, h1rr, TO_TR, 4 * part, 1)

    def top_left(s):
        for part in range(2):
            top_step(s - 3, s, 2, part, h1ls, h1lr, TO_TL, 8 + 3 * part, -1)

    def low_value(d):
        arrived(yr_s.at[near(d)], yrsem.at[near(d)])
        return part_s[near(d), y, SQ:, :] + yr_s[near(d)].astype(F32)

    def low_right(s):
        value = low_value(3 - s)
        if s:
            arrived(h2rr.at[s - 1], ersem.at[13 + s])
            value = value + h2rr[s - 1].astype(F32)
        h2rs[s] = value.astype(BF16)
        send(h2rs.at[s], h2rr.at[s], TO_LR, ersem.at[14 + s], ctx=right)

    def low_left(s):
        if s == 0:
            h2fs[...] = part_s[near(4), :, SQ:, :].astype(BF16)
            for yy in (y, 1 - y):
                send(h2fs.at[yy], h2fr.at[y], TO_LF, ersem.at[17], ctx=at_chip(-1, yy))
            return
        value = low_value(s - 4)
        if s == 1:
            arrived(h2fr, ersem.at[17])
            value = value + (h2fr[0].astype(F32) + h2fr[1].astype(F32))
        else:
            arrived(h2lr.at[s - 2], ersem.at[16 + s])
            value = value + h2lr[s - 2].astype(F32)
        h2ls[s - 1] = value.astype(BF16)
        send(h2ls.at[s - 1], h2lr.at[s - 1], TO_LL, ersem.at[17 + s], ctx=left)

    expand(4)
    top_right(0)
    low_left(0)
    expand(-3)
    top_left(0)
    for d in (3, -2, 2, -1, 1, 0):
        expand(d)
    for s in range(1, 4):
        top_right(s)
        low_left(s)
        if s < 3:
            top_left(s)
        low_right(s - 1)
    arrived(f1r, rsem.at[9])
    top_sum = part_s[z, y, :SQ, :] + f1r[...].astype(F32)
    ends = []
    for part in range(2):
        end = top_sum[PART * part : PART * (part + 1)]
        arrived(h1rr.at[3, part], ersem.at[4 * part + 3])
        arrived(h1lr.at[2, part], ersem.at[8 + 3 * part + 2])
        for yy in range(2):
            end = end + (h1rr[3, part, yy].astype(F32) + h1lr[2, part, yy].astype(F32))
        ends.append(end)
    low_sum = low_value(0)
    arrived(h2rr.at[2], ersem.at[16])
    arrived(h2lr.at[2], ersem.at[20])
    low_sum = low_sum + (h2rr[2].astype(F32) + h2lr[2].astype(F32))
    summed = (jnp.concatenate([*ends, low_sum], axis=0) * w_slot).astype(BF16)

    os_s[...] = dot(summed, take_sib).astype(BF16)
    push(os_s, or_s, ssem.at[10], rsem.at[10], ctx=sib)
    own_cols = dot(summed, take_own).astype(BF16)
    arrived(or_s, rsem.at[10])
    o_s[core] = own_cols
    o_s[1 - core] = or_s[...]
    slots = o_s[...].reshape(SLOTS, 256)
    terms = dot(tok_s[...], slots).reshape(EN, OUTR, 256)
    tails = pltpu.roll(terms[:, TOKB:, HD:].reshape(HALF, HD), 64, 1).reshape(EN, TOKB, HD)
    terms = jnp.concatenate([terms[:, :, :HD], terms[:, :TOKB, HD:] + tails], axis=1)
    town_s[...] = terms
    ts_s[...] = terms.astype(BF16)
    for d in range(1, EN):
        to = (e + d) % EN
        send(ts_s.at[to], tr_s.at[e], TO_TOK, prsem.at[2], ex=to)
    arrived(rr_s, rsem.at[8])
    resid = jnp.where(core == e // 4, resid_own, rr_s[...].astype(F32))
    mixed = town_s[e]
    arrived(tr_s.at[pl.ds(0, EN - 1)], prsem.at[2])
    for d in range(1, EN):
        mixed = mixed + tr_s[(e + d) % EN].astype(F32)
    tail = mixed[OUTR:]
    tail = jnp.concatenate([tail, pltpu.roll(tail, 64, 1)], axis=0)
    mixed = jnp.concatenate([mixed[:OUTR], tail], axis=1) + resid
    out_ref[...] = mixed[:, :COLS].astype(BF16)
    for copy in sent:
        copy.wait_send()
    for ref, kind in (
        (sib_s, TO_SIB), (num_s.at[pl.ds(0, ZN)], TO_Y), (num_s.at[pl.ds(ZN, ZN - 1)], TO_Z),
        (att_s.at[pl.ds(0, CHIPS - 1)], TO_CHIPS), (ps_s.at[pl.ds(0, EN - 1)], TO_EXP),
        (st_s.at[pl.ds(0, EN - 1)], TO_EXP_ALL), (x_s.at[:, 0, low_half, :], TO_LOW_Y),
        (x_s.at[pl.ds(0, 5), 0, low_half, :], TO_FIRST), (x_s.at[pl.ds(0, 5), 0], TO_PAIRS),
        (x_s.at[pl.ds(0, 7), 0, low_half, :], TO_LOW), (ys_s.at[pl.ds(0, ZN - 1)], TO_SUM_Y),
        (h1rs, TO_TR), (h1ls, TO_TL), (h2rs, TO_LR), (h2fs, TO_LF), (h2ls, TO_LL),
        (ts_s.at[pl.ds(0, EN - 1)], TO_TOK),
    ):
        left_here(ref, kind)


def local(hidden_in, queries, keys, values, out_weight, norm_gain, expert_gate, expert_up, expert_down, expert_ids, route_weights):
    vmem = pl.BlockSpec(memory_space=pltpu.VMEM)
    anywhere = pl.BlockSpec(memory_space=pltpu.HBM)
    dma = pltpu.SemaphoreType.DMA

    def buf(*shape, dtype=BF16):
        return pltpu.VMEM(shape, dtype)

    scratch = [
        buf(2, Q, dtype=jnp.int32), buf(2, Q, dtype=F32), buf(1, D, dtype=F32),
        buf(Q, HEADS * HD), buf(BLK, HD), buf(BLK, HD), buf(2, COLS, HALF),
        buf(2, COLS, HEADS * HD),
        buf(2, D, FF), buf(2, D, FF), buf(2, FF, D),
        buf(CHIPS, MSG, HD), buf(CHIPS, MSG, HD), buf(CHIPS, MSG, HD),
        buf(ZN, MSG, HD), buf(CHIPS, MSG, HD), buf(ZN, MSG, HD), buf(MSG, HD), buf(CHIPS, PAIRS, HD),
        buf(EN, TOKB, WIDE), buf(EN, TOKB, WIDE), buf(TOKB, WIDE, dtype=F32), buf(EN, TOKB, WIDE),
        buf(SH, WIDE), buf(SH, WIDE), buf(ZN, 2, SH, WIDE),
        buf(2, 2, SH, FF, dtype=F32), buf(SH, 128, dtype=F32), buf(ZN, 2, SH, WIDE, dtype=F32),
        buf(ZN, SQ, WIDE), buf(ZN, SQ, WIDE),
        buf(4, 2, 2, SQ // 2, WIDE), buf(4, 2, 2, SQ // 2, WIDE), buf(3, 2, 2, SQ // 2, WIDE), buf(3, 2, 2, SQ // 2, WIDE),
        buf(3, SQ, WIDE), buf(3, SQ, WIDE), buf(3, SQ, WIDE), buf(3, SQ, WIDE),
        buf(2, SQ, WIDE), buf(2, SQ, WIDE), buf(SQ, WIDE), buf(SQ, WIDE),
        buf(2, SH, 256), buf(SH, 256), buf(SH, 256), buf(OUTR, 256), buf(OUTR, 256),
        buf(EN, PACK, HD), buf(EN, PACK, HD), buf(EN, PACK, HD, dtype=F32), buf(Q, SLOTS),
        dma((11,)), dma((11,)), dma((11,)), dma((17,)), dma((4,)), dma((ZN,)), dma((1,)), dma((CHIPS,)),
        dma((3,)), dma((ZN,)), dma((ZN,)), dma((23,)), dma((21,)),
    ]
    return pl.pallas_call(
        layer_kernel,
        out_shape=jax.ShapeDtypeStruct((OUTR, COLS), BF16),
        in_specs=[anywhere] * 11,
        out_specs=vmem,
        scratch_shapes=scratch,
        compiler_params=pltpu.CompilerParams(
            collective_id=0, has_side_effects=True, vmem_limit_bytes=40 * 1024 * 1024
        ),
        cost_estimate=pl.CostEstimate(flops=3 * 10**9, bytes_accessed=12 * 10**6, transcendentals=2 * 10**6),
    )(
        *(
            pltpu.with_memory_space_constraint(x, pltpu.HBM)
            for x in (
                expert_ids.T, route_weights.T, norm_gain.reshape(1, D), queries, keys, values, hidden_in.T,
                out_weight.T, expert_gate, expert_up, expert_down,
            )
        )
    )


def solution(mesh):
    placed = (
        P(None, "ctx"),
        P(None, "exp"),
        P("ctx", "exp"),
        P("ctx", "exp"),
        P("exp", "ctx"),
        P(),
        P("exp", None, "ctx"),
        P("exp", None, "ctx"),
        P("exp", "ctx", None),
        P(),
        P(),
    )
    return jax.shard_map(
        local, mesh=mesh, in_specs=placed, out_specs=P("exp", "ctx"), check_vma=False
    )
```

```python
import functools
import math

import jax
import jax.numpy as jnp
from jax import lax
from jax.experimental import pallas as pl
from jax.experimental.pallas import tpu as pltpu
from jax.sharding import PartitionSpec as P

F32 = jnp.float32
BF16 = jnp.bfloat16
MESH = pl.DeviceIdType.MESH

HD = 128
D = 6144
Q = 512
CONTEXT = 16384
CHIPS = 16
ZN = 8
EN = 8
HEADS = 6
HALF = Q // 2
ROWS = HALF // CHIPS
PAIRS = ROWS * HEADS
BLK = 512
WIDE = 384
COLS = 192
SLOTS = 256
SH = SLOTS // 2
SQ = SH // 2
TOKB = HALF // EN
OUTR = Q // EN
FF = 256
PACK = OUTR + OUTR // 2
MSG = PAIRS + 16
GROUP = 4
PARTS = 2
PART = SQ // PARTS
AWAY = (4, -3, 3, -2, 2, -1, 1, 0)
FAR = AWAY[:3]


def dot(a, b, dims=((1,), (0,))):
    return lax.dot_general(a, b, (dims, ((), ())), preferred_element_type=F32)


def iota(shape, dim):
    return lax.broadcasted_iota(jnp.int32, shape, dim)


def layer_kernel(
    ids_hbm, rw_hbm, gain_hbm, q_hbm, k_hbm, v_hbm, hin_hbm, wout_hbm, gate_hbm, up_hbm, down_hbm,
    out_ref,
    ids_ref, rw_ref, gain_ref, q_s, k_s, v_s, h_s, w_s, gate_s, up_s, down_s,
    sib_s, sibr_s, part_o, yin_s, num_s, got_s, own_s, att_s, ps_s, pr_s, own_p, st_s,
    xs_s, xr_s, x_s, acc_s, sq_s, part_s, ys_s, yr_s,
    h1rs, h1rr, h1ls, h1lr, h2rs, h2rr, h2ls, h2lr, h2fs, h2fr, f1s, f1r,
    o_s, os_s, or_s, hot_s, take_s, ro_s, rs_s, rr_s, ts_s, tr_s, town_s, tok_s,
    lsem, ssem, rsem, tosem, krsem, vrsem, arsem, brsem, prsem, trsem, yrsem, xrsem, ersem,
):
    c = lax.axis_index("ctx")
    e = lax.axis_index("exp")
    core = c % 2
    chip = c // 2
    y = chip % 2
    z = chip // 2
    sib = c + 1 - 2 * core
    ypeer = c + 2 - 4 * y
    zp = [(z + d) % ZN for d in range(ZN)]

    def near(d):
        return zp[d % ZN]

    def at_chip(d, yy):
        return near(d) * 4 + yy * 2 + core

    right, left = at_chip(1, y), at_chip(-1, y)

    def owner(i):
        return near(AWAY[i % ZN]) * 2 + (1 - y if i < ZN else y)

    def remote(src, dst, send, recv, ctx=None, ex=None):
        return pltpu.make_async_remote_copy(
            src_ref=src, dst_ref=dst, send_sem=send, recv_sem=recv,
            device_id=(c if ctx is None else ctx, e if ex is None else ex),
            device_id_type=MESH,
        )

    def arrived(ref, sem):
        pltpu.make_async_copy(ref, ref, sem).wait()

    sent = []

    def push(*args, **kw):
        copy = remote(*args, **kw)
        copy.start()
        sent.append(copy)

    (TO_SIB, TO_Y, TO_Z, TO_CHIPS, TO_EXP, TO_EXP_ALL, TO_LOW_Y, TO_FIRST, TO_PAIRS, TO_LOW, TO_SUM_Y,
     TO_TR, TO_TL, TO_LR, TO_LF, TO_LL, TO_TOK) = range(17)

    def send(src, dst, kind, recv, **kw):
        remote(src, dst, tosem.at[kind], recv, **kw).start()

    def left_here(ref, kind):
        remote(ref, ref, tosem.at[kind], tosem.at[kind], ctx=sib).wait_send()

    barrier = pltpu.get_barrier_semaphore()

    def greet(ctx, ex):
        pl.semaphore_signal(barrier, inc=1, device_id=(ctx, ex), device_id_type=MESH)

    greet(sib, e)
    for d in range(1, CHIPS):
        greet(2 * ((chip + d) % CHIPS) + core, e)
    for d in range(1, EN):
        greet(c, (e + d) % EN)

    half_cols = pl.ds(pl.multiple_of(HALF * core, HALF), HALF)
    sib_cols = pl.ds(pl.multiple_of(HALF * (1 - core), HALF), HALF)
    gate_h, up_h, down_h = gate_hbm.at[0], up_hbm.at[0], down_hbm.at[0]
    loads = [
        pltpu.make_async_copy(k_hbm, k_s, lsem.at[0]),
        pltpu.make_async_copy(q_hbm, q_s, lsem.at[1]),
        pltpu.make_async_copy(v_hbm, v_s, lsem.at[2]),
        pltpu.make_async_copy(hin_hbm.at[:, half_cols], h_s.at[core], lsem.at[3]),
        pltpu.make_async_copy(wout_hbm, w_s.at[core], lsem.at[4]),
        pltpu.make_async_copy(gate_h, gate_s.at[core], lsem.at[5]),
        pltpu.make_async_copy(up_h, up_s.at[core], lsem.at[6]),
        pltpu.make_async_copy(down_h, down_s.at[core], lsem.at[7]),
        pltpu.make_async_copy(ids_hbm, ids_ref, lsem.at[8]),
        pltpu.make_async_copy(rw_hbm, rw_ref, lsem.at[9]),
        pltpu.make_async_copy(gain_hbm, gain_ref, lsem.at[10]),
    ]
    for load in loads:
        load.start()

    loads[0].wait()
    loads[1].wait()
    loads[2].wait()
    keys = k_s[...]
    vals = jnp.concatenate([v_s[...], jnp.ones((BLK, HD), BF16)], axis=1)
    diag = iota((PAIRS, HD), 0) == iota((PAIRS, HD), 1)
    stat_row = iota((16, HD), 0)

    def stats_block(pk, tt):
        pk0 = pk.astype(BF16).astype(F32)
        pk1 = (pk - pk0).astype(BF16).astype(F32)
        tt0 = tt.astype(BF16).astype(F32)
        stats = jnp.where(stat_row == 0, pk0, 0.0)
        for at, term in ((1, pk1), (2, pk - pk0 - pk1), (3, tt0), (4, tt - tt0)):
            stats = jnp.where(stat_row == at, term, stats)
        return stats.astype(BF16)

    def stats_of(block):
        stats = block[PAIRS:, :].astype(F32)
        return stats[0:1] + stats[1:2] + stats[2:3], stats[3:4] + stats[4:5]

    def as_column(row):
        return jnp.sum(jnp.where(diag, row, 0.0), axis=1, keepdims=True)

    def attend(half, into, start):
        first_limit = CONTEXT - Q - BLK * c
        rows, limits = [], []
        for i in range(start, start + GROUP):
            first = HALF * half + ROWS * owner(i)
            at = pl.ds(pl.multiple_of(first, ROWS), ROWS)
            for h in range(HEADS):
                rows.append(q_s[at, HD * h : HD * (h + 1)])
                limits.append(iota((ROWS, 1), 0) + (first_limit + first))
        qg = jnp.concatenate(rows, axis=0)
        limit = jnp.concatenate(limits, axis=0)
        scores = dot(qg, keys, ((1,), (1,))) * (math.log2(math.e) / math.sqrt(HD))
        scores = jnp.where(iota(scores.shape, 1) <= limit, scores, -1e30)
        peak = jnp.max(scores, axis=1, keepdims=True)
        both = dot(jnp.exp2(scores - peak).astype(BF16), vals)
        total = both[:, HD:]
        numer = (both[:, :HD] / total).astype(BF16)
        peaks = jnp.broadcast_to(peak, total.shape)
        for g in range(GROUP):
            part = slice(PAIRS * g, PAIRS * (g + 1))
            pk = jnp.sum(jnp.where(diag, peaks[part], 0.0), axis=0, keepdims=True)
            tt = jnp.sum(jnp.where(diag, total[part], 0.0), axis=0, keepdims=True)
            into[start + g, :PAIRS, :] = numer[part]
            into[start + g, PAIRS:, :] = stats_block(pk, tt)

    for start in range(0, CHIPS, GROUP):
        attend(1 - core, sib_s, start)
    for start in range(0, CHIPS, GROUP):
        attend(core, part_o, start)

    pl.semaphore_wait(barrier, 1 + (CHIPS - 1) + (EN - 1))

    for g in range(CHIPS // GROUP):
        some = pl.ds(GROUP * g, GROUP)
        send(sib_s.at[some], sibr_s.at[some], TO_SIB, krsem.at[g], ctx=sib)
    push(hin_hbm.at[:, sib_cols], h_s.at[core], ssem.at[2], rsem.at[2], ctx=sib)
    push(wout_hbm, w_s.at[core], ssem.at[3], rsem.at[3], ctx=sib)
    push(gate_h, gate_s.at[core], ssem.at[4], rsem.at[4], ctx=sib)
    push(up_h, up_s.at[core], ssem.at[5], rsem.at[5], ctx=sib)
    push(down_h, down_s.at[core], ssem.at[6], rsem.at[6], ctx=sib)

    def merge(blocks):
        stats = [stats_of(block) for block in blocks]
        top = functools.reduce(jnp.maximum, [pk for pk, _ in stats])
        factors = [jnp.exp2(pk - top) * tt for pk, tt in stats]
        whole = sum(factors[1:], factors[0])
        inverse = 1.0 / jnp.maximum(whole, 1e-30)
        terms = [as_column(f * inverse) * block[:PAIRS, :].astype(F32) for f, block in zip(factors, blocks)]
        return sum(terms[1:], terms[0]).astype(BF16), top, whole

    def write(into, merged):
        numer, top, whole = merged
        into[:PAIRS, :] = numer
        into[PAIRS:, :] = stats_block(top, whole)

    def sibling_arrived(i):
        if i % GROUP == 0:
            arrived(sibr_s.at[pl.ds(i, GROUP)], krsem.at[i // GROUP])

    for i in range(ZN):
        sibling_arrived(i)
        write(num_s.at[i], merge([part_o.at[i], sibr_s.at[i]]))
        send(num_s.at[i], yin_s.at[i], TO_Y, vrsem.at[i], ctx=ypeer)
    for i in range(ZN):
        sibling_arrived(ZN + i)
        arrived(yin_s.at[i], vrsem.at[i])
        merged = merge([part_o.at[ZN + i], sibr_s.at[ZN + i], yin_s.at[i]])
        if AWAY[i]:
            write(num_s.at[ZN + i], merged)
            send(num_s.at[ZN + i], got_s.at[z], TO_Z, arsem.at[0], ctx=at_chip(AWAY[i], y))
        else:
            write(own_s, merged)

    loads[8].wait()
    loads[9].wait()
    ids = ids_ref[...]
    owned = jnp.where((ids[0:1] == e) | (ids[1:2] == e), 1.0, 0.0)
    w_row = jnp.where(ids[0:1] == e, rw_ref[0:1, :], 0.0) + jnp.where(ids[1:2] == e, rw_ref[1:2, :], 0.0)
    before = jnp.where(iota((Q, Q), 0) < iota((Q, Q), 1), 1.0, 0.0).astype(BF16)
    rank = dot(jnp.broadcast_to(owned, (16, Q)).astype(BF16), before)[0:1]
    place = jnp.where(owned > 0.5, rank, -1.0)
    place_col = jnp.transpose(jnp.broadcast_to(place, (HD, Q)))
    for part in range(2):
        lane = (iota((Q, SH), 1) + SH * part).astype(F32)
        tok_s[:, SH * part : SH * (part + 1)] = jnp.where(place_col == lane, 1.0, 0.0).astype(BF16)
    slot_own = (iota((SH, Q), 0) + SH * core).astype(F32)
    w_slot = jnp.sum(jnp.where(place == slot_own, w_row, 0.0), axis=1, keepdims=True)

    here = jnp.where(core == 0, place[:, :HALF], place[:, HALF:])
    for part in range(2):
        pick = (iota((SH, HALF), 0) + SH * part).astype(F32)
        hot_s[part] = jnp.where(here == pick, 1.0, 0.0).astype(BF16)

    arrived(got_s.at[pl.ds(0, ZN - 1)], arsem.at[0])
    att_s[chip] = merge([own_s] + [got_s.at[near(d)] for d in AWAY[:-1]])[0]
    for d in AWAY:
        for yy in (y, 1 - y):
            if yy is y and d == 0 or yy is not y and d in FAR:
                continue
            send(att_s.at[chip], att_s.at[chip], TO_CHIPS, brsem.at[chip], ctx=at_chip(d, yy))
    for d in FAR:
        source = 2 * near(d) + y
        arrived(att_s.at[source], brsem.at[source])
        send(att_s.at[source], att_s.at[source], TO_CHIPS, brsem.at[source], ctx=ypeer)

    loads[4].wait()
    arrived(w_s.at[1 - core], rsem.at[3])
    weight = w_s[...].reshape(WIDE, HEADS * HD)
    for d in (0, *AWAY[3:-1], *FAR):
        to = near(d)
        for source in (2 * to, 2 * to + 1) if d and d not in FAR else (2 * to + 1 - y,):
            arrived(att_s.at[source], brsem.at[source])
        pair = att_s[pl.ds(2 * to, 2)]
        attended = jnp.concatenate(
            [pair[:, ROWS * h : ROWS * (h + 1), :].reshape(TOKB, HD) for h in range(HEADS)], axis=1
        )
        projected = dot(attended, weight, ((1,), (1,)))
        ps_s[to] = projected.astype(BF16)

        @pl.when(to == e)
        def _(projected=projected):
            own_p[...] = projected

        @pl.when(to != e)
        def _(to=to):
            send(ps_s.at[to], pr_s.at[e], TO_EXP, prsem.at[0], ex=to)

    loads[3].wait()
    arrived(h_s.at[1 - core], rsem.at[2])
    my_tokens = jnp.where(iota((TOKB, HALF), 1) == iota((TOKB, HALF), 0) + TOKB * e, 1.0, 0.0).astype(BF16)
    before_attention = dot(my_tokens, h_s[...].reshape(WIDE, HALF), ((1,), (1,)))
    stream = own_p[...]
    arrived(pr_s.at[pl.ds(0, EN - 1)], prsem.at[0])
    for d in range(1, EN):
        source = (e + d) % EN
        stream = stream + pr_s[source].astype(F32)
    stream = stream + before_attention
    st_s[e] = stream.astype(BF16)
    for d in range(1, EN):
        to = (e + d) % EN
        send(st_s.at[e], st_s.at[e], TO_EXP_ALL, prsem.at[1], ex=to)
    arrived(st_s.at[pl.ds(0, EN - 1)], prsem.at[1])

    rows = st_s[...].reshape(HALF, WIDE)

    xs_s[...] = dot(hot_s[1 - core], rows).astype(BF16)
    push(xs_s, xr_s, ssem.at[7], rsem.at[7], ctx=sib)
    mine = dot(hot_s[core], rows)
    arrived(xr_s, rsem.at[7])
    x_s[z, y] = (mine + xr_s[...].astype(F32)).astype(BF16)

    low_half = pl.ds(SQ, SQ)

    def x_low(d, yy):
        return x_s.at[near(d), yy, low_half, :]

    def x_top(d, part):
        return x_s.at[near(d), :, pl.ds(PART * part, PART), :]

    def x_one(d, yy, part):
        return x_s.at[near(d), yy, pl.ds(PART * part, PART), :]

    FR, FL, OY = 0, PARTS, 2 * PARTS
    TR = [3 * PARTS + 3 * part for part in range(PARTS)]
    TL = [6 * PARTS + 2 * part for part in range(PARTS)]
    LR, LL = 8 * PARTS, 8 * PARTS + 3

    def same(block, kind, recv, to):
        send(block, block, kind, recv, ctx=to)

    def first_hops(part, base, d):
        for yy in (y, 1 - y):
            same(x_one(0, y, part), TO_FIRST, xrsem.at[base + part], at_chip(d, yy))

    same(x_low(0, y), TO_LOW, xrsem.at[LL], left)
    for part in range(PARTS):
        first_hops(part, FR, 1)
        first_hops(part, FL, -1)
    same(x_low(0, y), TO_LOW, xrsem.at[LR], right)
    same(x_low(0, y), TO_LOW_Y, trsem.at[z], ypeer)
    for part in range(PARTS):
        same(x_one(0, y, part), TO_FIRST, xrsem.at[OY + part], ypeer)

    resid = st_s[pl.ds(2 * (e % 4), 2)].reshape(OUTR, WIDE)
    take_own = jnp.where(iota((WIDE, 256), 0) == iota((WIDE, 256), 1) + COLS * core, 1.0, 0.0)
    take_sib = jnp.where(iota((WIDE, 256), 0) == iota((WIDE, 256), 1) + COLS * (1 - core), 1.0, 0.0)
    valid = iota((WIDE, 256), 1) < COLS
    take_s[0] = jnp.where(valid, take_own, 0.0).astype(BF16)
    take_s[1] = jnp.where(valid, take_sib, 0.0).astype(BF16)
    rs_s[...] = dot(resid, take_s[1]).astype(BF16)
    push(rs_s, rr_s, ssem.at[8], rsem.at[8], ctx=sib)
    ro_s[...] = dot(resid, take_s[0])

    loads[5].wait()
    loads[6].wait()
    loads[10].wait()
    arrived(gate_s.at[1 - core], rsem.at[4])
    arrived(up_s.at[1 - core], rsem.at[5])
    acc_s[...] = jnp.zeros_like(acc_s)
    sq_s[...] = jnp.zeros_like(sq_s)

    def project(d):
        zz = near(d)
        for yy in range(2):
            at = pl.ds(pl.multiple_of(WIDE * (2 * zz + yy), WIDE), WIDE)
            block = x_s[zz, yy].astype(F32)
            square = block * block
            sq_s[...] += square[:, :128] + square[:, 128:256] + square[:, 256:]
            scaled = (block * gain_ref[:, at]).astype(BF16)
            for kk in range(2):
                acc_s[0, kk] += dot(scaled, gate_s[kk, at, :])
                acc_s[1, kk] += dot(scaled, up_s[kk, at, :])

    def low_arrived(d):
        arrived(x_low(d, 1 - y), trsem.at[near(d)])

    def top_on(d, s, part, first, base, last, to):
        arrived(x_top(d, part), xrsem.at[first + part if s == 1 else base[part] + s - 2])
        if s < last:
            same(x_top(d, part), TO_PAIRS, xrsem.at[base[part] + s - 1], to)

    def low_on(d, s, base, last, to):
        block = x_low(d, y)
        arrived(block, xrsem.at[base + s - 1])
        if s < last:
            same(block, TO_LOW, xrsem.at[base + s], to)
        if s <= 3:
            same(block, TO_LOW_Y, trsem.at[near(d)], ypeer)
        if d == 3:
            same(block, TO_LOW_Y, trsem.at[near(d)], at_chip(-1, 1 - y))

    for s in range(1, 5):
        low_on(s, s, LL, 4, left)
        for part in range(PARTS):
            top_on(-s, s, part, FR, TR, 4, right)
            if s <= 3:
                top_on(s, s, part, FL, TL, 3, left)
        if s <= 3:
            low_on(-s, s, LR, 3, right)
        if s == 1:
            for part in range(PARTS):
                arrived(x_one(0, 1 - y, part), xrsem.at[OY + part])
            low_arrived(0)
            project(0)
        else:
            low_arrived(s - 1)
            project(s - 1)
            low_arrived(1 - s)
            project(1 - s)
    low_arrived(4)
    project(4)

    inverse_rms = lax.rsqrt(jnp.sum(sq_s[...], axis=1, keepdims=True) / D + 1e-5)
    hidden = []
    for kk in range(2):
        gate_val = acc_s[0, kk] * inverse_rms
        up_val = acc_s[1, kk] * inverse_rms
        hidden.append((gate_val / (1.0 + jnp.exp(-gate_val)) * up_val).astype(BF16))
    loads[7].wait()
    arrived(down_s.at[1 - core], rsem.at[6])

    def expand(d):
        zz = near(d)
        for yy in range(2):
            at = pl.ds(pl.multiple_of(WIDE * (2 * zz + yy), WIDE), WIDE)
            part_s[zz, yy] = dot(hidden[0], down_s[0, :, at]) + dot(hidden[1], down_s[1, :, at])
        if d == 0:
            f1s[...] = part_s[zz, 1 - y, :SQ, :].astype(BF16)
            push(f1s, f1r, ssem.at[9], rsem.at[9], ctx=ypeer)
        if d != 4:
            ys_s[zz] = part_s[zz, 1 - y, SQ:, :].astype(BF16)
            send(ys_s.at[zz], yr_s.at[zz], TO_SUM_Y, yrsem.at[zz], ctx=ypeer)

    LR, LL = 7 * PARTS, 7 * PARTS + 3

    def top_step(d, s, last, part, out_s, in_s, kind, base, step):
        value = part_s[near(d), :, PART * part : PART * (part + 1), :]
        if s:
            arrived(in_s.at[s - 1, part], ersem.at[base + s - 1])
            value = value + in_s[s - 1, part].astype(F32)
        out_s[s, part] = value.astype(BF16)
        if s < last:
            send(out_s.at[s, part], in_s.at[s, part], kind, ersem.at[base + s], ctx=at_chip(step, y))
        else:
            for yy in (y, 1 - y):
                send(out_s.at[s, part, yy], in_s.at[s, part, y], kind, ersem.at[base + s], ctx=at_chip(step, yy))

    def top_right(s):
        for part in range(PARTS):
            top_step(4 - s, s, 3, part, h1rs, h1rr, TO_TR, 4 * part, 1)

    def top_left(s):
        for part in range(PARTS):
            top_step(s - 3, s, 2, part, h1ls, h1lr, TO_TL, 4 * PARTS + 3 * part, -1)

    def low_value(d):
        arrived(yr_s.at[near(d)], yrsem.at[near(d)])
        return part_s[near(d), y, SQ:, :] + yr_s[near(d)].astype(F32)

    def low_right(s):
        value = low_value(3 - s)
        if s:
            arrived(h2rr.at[s - 1], ersem.at[LR + s - 1])
            value = value + h2rr[s - 1].astype(F32)
        h2rs[s] = value.astype(BF16)
        send(h2rs.at[s], h2rr.at[s], TO_LR, ersem.at[LR + s], ctx=right)

    def low_left(s):
        if s == 0:
            h2fs[...] = part_s[near(4), :, SQ:, :].astype(BF16)
            for yy in (y, 1 - y):
                send(h2fs.at[yy], h2fr.at[y], TO_LF, ersem.at[LL], ctx=at_chip(-1, yy))
            return
        value = low_value(s - 4)
        if s == 1:
            arrived(h2fr, ersem.at[LL])
            value = value + (h2fr[0].astype(F32) + h2fr[1].astype(F32))
        else:
            arrived(h2lr.at[s - 2], ersem.at[LL + s - 1])
            value = value + h2lr[s - 2].astype(F32)
        h2ls[s - 1] = value.astype(BF16)
        send(h2ls.at[s - 1], h2lr.at[s - 1], TO_LL, ersem.at[LL + s], ctx=left)

    expand(4)
    top_right(0)
    low_left(0)
    expand(3)
    expand(-3)
    top_left(0)
    for d in (-2, 2, -1, 1):
        expand(d)
    for s in range(1, 4):
        top_right(s)
        low_right(s - 1)
        low_left(s)
        if s < 3:
            top_left(s)
        if s == 2:
            expand(0)
    arrived(f1r, rsem.at[9])
    top_sum = part_s[z, y, :SQ, :] + f1r[...].astype(F32)
    ends = []
    for part in range(PARTS):
        end = top_sum[PART * part : PART * (part + 1)]
        arrived(h1rr.at[3, part], ersem.at[4 * part + 3])
        arrived(h1lr.at[2, part], ersem.at[4 * PARTS + 3 * part + 2])
        for yy in range(2):
            end = end + (h1rr[3, part, yy].astype(F32) + h1lr[2, part, yy].astype(F32))
        ends.append(end)
    low_sum = low_value(0)
    arrived(h2rr.at[2], ersem.at[LR + 2])
    arrived(h2lr.at[2], ersem.at[LL + 3])
    low_sum = low_sum + (h2rr[2].astype(F32) + h2lr[2].astype(F32))
    summed = (jnp.concatenate([*ends, low_sum], axis=0) * w_slot).astype(BF16)

    os_s[...] = dot(summed, take_s[1]).astype(BF16)
    push(os_s, or_s, ssem.at[10], rsem.at[10], ctx=sib)
    own_cols = dot(summed, take_s[0]).astype(BF16)
    arrived(or_s, rsem.at[10])
    o_s[core] = own_cols
    o_s[1 - core] = or_s[...]
    slots = o_s[...].reshape(SLOTS, 256)
    terms = dot(tok_s[...], slots).reshape(EN, OUTR, 256)
    tails = pltpu.roll(terms[:, TOKB:, HD:].reshape(HALF, HD), 64, 1).reshape(EN, TOKB, HD)
    terms = jnp.concatenate([terms[:, :, :HD], terms[:, :TOKB, HD:] + tails], axis=1)
    town_s[...] = terms
    ts_s[...] = terms.astype(BF16)
    for d in range(1, EN):
        to = (e + d) % EN
        send(ts_s.at[to], tr_s.at[e], TO_TOK, prsem.at[2], ex=to)
    arrived(rr_s, rsem.at[8])
    resid = jnp.where(core == e // 4, ro_s[...], rr_s[...].astype(F32))
    mixed = town_s[e]
    arrived(tr_s.at[pl.ds(0, EN - 1)], prsem.at[2])
    for d in range(1, EN):
        mixed = mixed + tr_s[(e + d) % EN].astype(F32)
    tail = mixed[OUTR:]
    tail = jnp.concatenate([tail, pltpu.roll(tail, 64, 1)], axis=0)
    mixed = jnp.concatenate([mixed[:OUTR], tail], axis=1) + resid
    out_ref[...] = mixed[:, :COLS].astype(BF16)
    for copy in sent:
        copy.wait_send()
    for ref, kind in (
        (sib_s, TO_SIB), (num_s.at[pl.ds(0, ZN)], TO_Y), (num_s.at[pl.ds(ZN, ZN - 1)], TO_Z),
        (att_s.at[pl.ds(0, CHIPS - 1)], TO_CHIPS), (ps_s.at[pl.ds(0, EN - 1)], TO_EXP),
        (st_s.at[pl.ds(0, EN - 1)], TO_EXP_ALL), (x_s.at[:, 0, low_half, :], TO_LOW_Y),
        (x_s.at[pl.ds(0, 5), 0, low_half, :], TO_FIRST), (x_s.at[pl.ds(0, 5), 0], TO_PAIRS),
        (x_s.at[pl.ds(0, 7), 0, low_half, :], TO_LOW), (ys_s.at[pl.ds(0, ZN - 1)], TO_SUM_Y),
        (h1rs, TO_TR), (h1ls, TO_TL), (h2rs, TO_LR), (h2fs, TO_LF), (h2ls, TO_LL),
        (ts_s.at[pl.ds(0, EN - 1)], TO_TOK),
    ):
        left_here(ref, kind)


def local(hidden_in, queries, keys, values, out_weight, norm_gain, expert_gate, expert_up, expert_down, expert_ids, route_weights):
    vmem = pl.BlockSpec(memory_space=pltpu.VMEM)
    anywhere = pl.BlockSpec(memory_space=pltpu.HBM)
    dma = pltpu.SemaphoreType.DMA

    def buf(*shape, dtype=BF16):
        return pltpu.VMEM(shape, dtype)

    scratch = [
        buf(2, Q, dtype=jnp.int32), buf(2, Q, dtype=F32), buf(1, D, dtype=F32),
        buf(Q, HEADS * HD), buf(BLK, HD), buf(BLK, HD), buf(2, COLS, HALF),
        buf(2, COLS, HEADS * HD),
        buf(2, D, FF), buf(2, D, FF), buf(2, FF, D),
        buf(CHIPS, MSG, HD), buf(CHIPS, MSG, HD), buf(CHIPS, MSG, HD),
        buf(ZN, MSG, HD), buf(CHIPS, MSG, HD), buf(ZN, MSG, HD), buf(MSG, HD), buf(CHIPS, PAIRS, HD),
        buf(EN, TOKB, WIDE), buf(EN, TOKB, WIDE), buf(TOKB, WIDE, dtype=F32), buf(EN, TOKB, WIDE),
        buf(SH, WIDE), buf(SH, WIDE), buf(ZN, 2, SH, WIDE),
        buf(2, 2, SH, FF, dtype=F32), buf(SH, 128, dtype=F32), buf(ZN, 2, SH, WIDE, dtype=F32),
        buf(ZN, SQ, WIDE), buf(ZN, SQ, WIDE),
        buf(4, PARTS, 2, PART, WIDE), buf(4, PARTS, 2, PART, WIDE), buf(3, PARTS, 2, PART, WIDE), buf(3, PARTS, 2, PART, WIDE),
        buf(3, SQ, WIDE), buf(3, SQ, WIDE), buf(3, SQ, WIDE), buf(3, SQ, WIDE),
        buf(2, SQ, WIDE), buf(2, SQ, WIDE), buf(SQ, WIDE), buf(SQ, WIDE),
        buf(2, SH, 256), buf(SH, 256), buf(SH, 256), buf(2, SH, HALF), buf(2, WIDE, 256), buf(OUTR, 256, dtype=F32), buf(OUTR, 256), buf(OUTR, 256),
        buf(EN, PACK, HD), buf(EN, PACK, HD), buf(EN, PACK, HD, dtype=F32), buf(Q, SLOTS),
        dma((11,)), dma((11,)), dma((11,)), dma((17,)), dma((4,)), dma((ZN,)), dma((1,)), dma((CHIPS,)),
        dma((3,)), dma((ZN,)), dma((ZN,)), dma((8 * PARTS + 7,)), dma((7 * PARTS + 7,)),
    ]
    return pl.pallas_call(
        layer_kernel,
        out_shape=jax.ShapeDtypeStruct((OUTR, COLS), BF16),
        in_specs=[anywhere] * 11,
        out_specs=vmem,
        scratch_shapes=scratch,
        compiler_params=pltpu.CompilerParams(
            collective_id=0, has_side_effects=True, vmem_limit_bytes=40 * 1024 * 1024
        ),
        cost_estimate=pl.CostEstimate(flops=3 * 10**9, bytes_accessed=12 * 10**6, transcendentals=2 * 10**6),
    )(
        *(
            pltpu.with_memory_space_constraint(x, pltpu.HBM)
            for x in (
                expert_ids.T, route_weights.T, norm_gain.reshape(1, D), queries, keys, values, hidden_in.T,
                out_weight.T, expert_gate, expert_up, expert_down,
            )
        )
    )


def solution(mesh):
    placed = (
        P(None, "ctx"),
        P(None, "exp"),
        P("ctx", "exp"),
        P("ctx", "exp"),
        P("exp", "ctx"),
        P(),
        P("exp", None, "ctx"),
        P("exp", None, "ctx"),
        P("exp", "ctx", None),
        P(),
        P(),
    )
    return jax.shard_map(
        local, mesh=mesh, in_specs=placed, out_specs=P("exp", "ctx"), check_vma=False
    )
```

```python
import functools
import math

import jax
import jax.numpy as jnp
from jax import lax
from jax.experimental import pallas as pl
from jax.experimental.pallas import tpu as pltpu
from jax.sharding import PartitionSpec as P

F32 = jnp.float32
BF16 = jnp.bfloat16
MESH = pl.DeviceIdType.MESH

HD = 128
D = 6144
Q = 512
CONTEXT = 16384
CHIPS = 16
ZN = 8
EN = 8
HEADS = 6
HALF = Q // 2
ROWS = HALF // CHIPS
PAIRS = ROWS * HEADS
BLK = 512
WIDE = 384
COLS = 192
SLOTS = 256
SH = SLOTS // 2
SQ = SH // 2
TOKB = HALF // EN
OUTR = Q // EN
FF = 256
PACK = OUTR + OUTR // 2
MSG = PAIRS + 16
EXP_FAR = (5, 3, 7, 1, 4, 2, 6)
GROUP = 4
PARTS = 2
PART = SQ // PARTS
AWAY = (4, -3, 3, -2, 2, -1, 1, 0)
FAR = AWAY[:3]


def dot(a, b, dims=((1,), (0,))):
    return lax.dot_general(a, b, (dims, ((), ())), preferred_element_type=F32)


def iota(shape, dim):
    return lax.broadcasted_iota(jnp.int32, shape, dim)


def layer_kernel(
    ids_hbm, rw_hbm, gain_hbm, q_hbm, k_hbm, v_hbm, hin_hbm, wout_hbm, gate_hbm, up_hbm, down_hbm,
    out_ref,
    ids_ref, rw_ref, gain_ref, q_s, k_s, v_s, h_s, w_s, gate_s, up_s, down_s,
    sib_s, sibr_s, part_o, yin_s, num_s, got_s, own_s, att_s, ps_s, pr_s, own_p, st_s,
    xs_s, xr_s, x_s, acc_s, sq_s, part_s, ys_s, yr_s,
    h1rs, h1rr, h1ls, h1lr, h2rs, h2rr, h2ls, h2lr, h2fs, h2fr, f1s, f1r,
    o_s, os_s, or_s, hot_s, take_s, ro_s, rs_s, rr_s, ts_s, tr_s, town_s, tok_s,
    lsem, ssem, rsem, tosem, krsem, vrsem, arsem, brsem, prsem, trsem, yrsem, xrsem, ersem,
):
    c = lax.axis_index("ctx")
    e = lax.axis_index("exp")
    core = c % 2
    chip = c // 2
    y = chip % 2
    z = chip // 2
    sib = c + 1 - 2 * core
    ypeer = c + 2 - 4 * y
    zp = [(z + d) % ZN for d in range(ZN)]

    def near(d):
        return zp[d % ZN]

    def at_chip(d, yy):
        return near(d) * 4 + yy * 2 + core

    right, left = at_chip(1, y), at_chip(-1, y)

    def owner(i):
        return near(AWAY[i % ZN]) * 2 + (1 - y if i < ZN else y)

    def remote(src, dst, send, recv, ctx=None, ex=None):
        return pltpu.make_async_remote_copy(
            src_ref=src, dst_ref=dst, send_sem=send, recv_sem=recv,
            device_id=(c if ctx is None else ctx, e if ex is None else ex),
            device_id_type=MESH,
        )

    def arrived(ref, sem):
        pltpu.make_async_copy(ref, ref, sem).wait()

    sent = []

    def push(*args, **kw):
        copy = remote(*args, **kw)
        copy.start()
        sent.append(copy)

    (TO_SIB, TO_Y, TO_Z, TO_CHIPS, TO_EXP, TO_EXP_ALL, TO_LOW_Y, TO_FIRST, TO_PAIRS, TO_LOW, TO_SUM_Y,
     TO_TR, TO_TL, TO_LR, TO_LF, TO_LL, TO_TOK) = range(17)

    def send(src, dst, kind, recv, **kw):
        remote(src, dst, tosem.at[kind], recv, **kw).start()

    def left_here(ref, kind):
        remote(ref, ref, tosem.at[kind], tosem.at[kind], ctx=sib).wait_send()

    barrier = pltpu.get_barrier_semaphore()

    def greet(ctx, ex):
        pl.semaphore_signal(barrier, inc=1, device_id=(ctx, ex), device_id_type=MESH)

    greet(sib, e)
    for d in range(1, CHIPS):
        greet(2 * ((chip + d) % CHIPS) + core, e)
    for d in range(1, EN):
        greet(c, (e + d) % EN)

    half_cols = pl.ds(pl.multiple_of(HALF * core, HALF), HALF)
    sib_cols = pl.ds(pl.multiple_of(HALF * (1 - core), HALF), HALF)
    gate_h, up_h, down_h = gate_hbm.at[0], up_hbm.at[0], down_hbm.at[0]
    loads = [
        pltpu.make_async_copy(k_hbm, k_s, lsem.at[0]),
        pltpu.make_async_copy(q_hbm, q_s, lsem.at[1]),
        pltpu.make_async_copy(v_hbm, v_s, lsem.at[2]),
        pltpu.make_async_copy(hin_hbm.at[:, half_cols], h_s.at[core], lsem.at[3]),
        pltpu.make_async_copy(wout_hbm, w_s.at[core], lsem.at[4]),
        pltpu.make_async_copy(gate_h, gate_s.at[core], lsem.at[5]),
        pltpu.make_async_copy(up_h, up_s.at[core], lsem.at[6]),
        pltpu.make_async_copy(down_h, down_s.at[core], lsem.at[7]),
        pltpu.make_async_copy(ids_hbm, ids_ref, lsem.at[8]),
        pltpu.make_async_copy(rw_hbm, rw_ref, lsem.at[9]),
        pltpu.make_async_copy(gain_hbm, gain_ref, lsem.at[10]),
    ]
    for load in loads:
        load.start()

    loads[0].wait()
    loads[1].wait()
    loads[2].wait()
    keys = k_s[...]
    vals = jnp.concatenate([v_s[...], jnp.ones((BLK, HD), BF16)], axis=1)
    diag = iota((PAIRS, HD), 0) == iota((PAIRS, HD), 1)
    stat_row = iota((16, HD), 0)

    def stats_block(pk, tt):
        pk0 = pk.astype(BF16).astype(F32)
        pk1 = (pk - pk0).astype(BF16).astype(F32)
        tt0 = tt.astype(BF16).astype(F32)
        stats = jnp.where(stat_row == 0, pk0, 0.0)
        for at, term in ((1, pk1), (2, pk - pk0 - pk1), (3, tt0), (4, tt - tt0)):
            stats = jnp.where(stat_row == at, term, stats)
        return stats.astype(BF16)

    def stats_of(block):
        stats = block[PAIRS:, :].astype(F32)
        return stats[0:1] + stats[1:2] + stats[2:3], stats[3:4] + stats[4:5]

    def as_column(row):
        return jnp.sum(jnp.where(diag, row, 0.0), axis=1, keepdims=True)

    def attend(half, into, start):
        first_limit = CONTEXT - Q - BLK * c
        rows, limits = [], []
        for i in range(start, start + GROUP):
            first = HALF * half + ROWS * owner(i)
            at = pl.ds(pl.multiple_of(first, ROWS), ROWS)
            for h in range(HEADS):
                rows.append(q_s[at, HD * h : HD * (h + 1)])
                limits.append(iota((ROWS, 1), 0) + (first_limit + first))
        qg = jnp.concatenate(rows, axis=0)
        limit = jnp.concatenate(limits, axis=0)
        scores = dot(qg, keys, ((1,), (1,))) * (math.log2(math.e) / math.sqrt(HD))
        scores = jnp.where(iota(scores.shape, 1) <= limit, scores, -1e30)
        peak = jnp.max(scores, axis=1, keepdims=True)
        both = dot(jnp.exp2(scores - peak).astype(BF16), vals)
        total = both[:, HD:]
        numer = (both[:, :HD] / total).astype(BF16)
        peaks = jnp.broadcast_to(peak, total.shape)
        for g in range(GROUP):
            part = slice(PAIRS * g, PAIRS * (g + 1))
            pk = jnp.sum(jnp.where(diag, peaks[part], 0.0), axis=0, keepdims=True)
            tt = jnp.sum(jnp.where(diag, total[part], 0.0), axis=0, keepdims=True)
            into[start + g, :PAIRS, :] = numer[part]
            into[start + g, PAIRS:, :] = stats_block(pk, tt)

    for start in range(0, CHIPS, GROUP):
        attend(1 - core, sib_s, start)
    for start in range(0, CHIPS, GROUP):
        attend(core, part_o, start)

    pl.semaphore_wait(barrier, 1 + (CHIPS - 1) + (EN - 1))

    for g in range(CHIPS // GROUP):
        some = pl.ds(GROUP * g, GROUP)
        send(sib_s.at[some], sibr_s.at[some], TO_SIB, krsem.at[g], ctx=sib)
    push(hin_hbm.at[:, sib_cols], h_s.at[core], ssem.at[2], rsem.at[2], ctx=sib)
    push(wout_hbm, w_s.at[core], ssem.at[3], rsem.at[3], ctx=sib)
    push(gate_h, gate_s.at[core], ssem.at[4], rsem.at[4], ctx=sib)
    push(up_h, up_s.at[core], ssem.at[5], rsem.at[5], ctx=sib)
    push(down_h, down_s.at[core], ssem.at[6], rsem.at[6], ctx=sib)

    def merge(blocks):
        stats = [stats_of(block) for block in blocks]
        top = functools.reduce(jnp.maximum, [pk for pk, _ in stats])
        factors = [jnp.exp2(pk - top) * tt for pk, tt in stats]
        whole = sum(factors[1:], factors[0])
        inverse = 1.0 / jnp.maximum(whole, 1e-30)
        terms = [as_column(f * inverse) * block[:PAIRS, :].astype(F32) for f, block in zip(factors, blocks)]
        return sum(terms[1:], terms[0]).astype(BF16), top, whole

    def write(into, merged):
        numer, top, whole = merged
        into[:PAIRS, :] = numer
        into[PAIRS:, :] = stats_block(top, whole)

    def sibling_arrived(i):
        if i % GROUP == 0:
            arrived(sibr_s.at[pl.ds(i, GROUP)], krsem.at[i // GROUP])

    for i in range(ZN):
        sibling_arrived(i)
        write(num_s.at[i], merge([part_o.at[i], sibr_s.at[i]]))
        send(num_s.at[i], yin_s.at[i], TO_Y, vrsem.at[i], ctx=ypeer)
    for i in range(ZN):
        sibling_arrived(ZN + i)
        arrived(yin_s.at[i], vrsem.at[i])
        merged = merge([part_o.at[ZN + i], sibr_s.at[ZN + i], yin_s.at[i]])
        if AWAY[i]:
            write(num_s.at[ZN + i], merged)
            send(num_s.at[ZN + i], got_s.at[z], TO_Z, arsem.at[0], ctx=at_chip(AWAY[i], y))
        else:
            write(own_s, merged)

    loads[8].wait()
    loads[9].wait()
    ids = ids_ref[...]
    owned = jnp.where((ids[0:1] == e) | (ids[1:2] == e), 1.0, 0.0)
    w_row = jnp.where(ids[0:1] == e, rw_ref[0:1, :], 0.0) + jnp.where(ids[1:2] == e, rw_ref[1:2, :], 0.0)
    before = jnp.where(iota((Q, Q), 0) < iota((Q, Q), 1), 1.0, 0.0).astype(BF16)
    rank = dot(jnp.broadcast_to(owned, (16, Q)).astype(BF16), before)[0:1]
    place = jnp.where(owned > 0.5, rank, -1.0)
    place_col = jnp.transpose(jnp.broadcast_to(place, (HD, Q)))
    for part in range(2):
        lane = (iota((Q, SH), 1) + SH * part).astype(F32)
        tok_s[:, SH * part : SH * (part + 1)] = jnp.where(place_col == lane, 1.0, 0.0).astype(BF16)
    slot_own = (iota((SH, Q), 0) + SH * core).astype(F32)
    w_slot = jnp.sum(jnp.where(place == slot_own, w_row, 0.0), axis=1, keepdims=True)

    here = jnp.where(core == 0, place[:, :HALF], place[:, HALF:])
    for part in range(2):
        pick = (iota((SH, HALF), 0) + SH * part).astype(F32)
        hot_s[part] = jnp.where(here == pick, 1.0, 0.0).astype(BF16)

    arrived(got_s.at[pl.ds(0, ZN - 1)], arsem.at[0])
    att_s[chip] = merge([own_s] + [got_s.at[near(d)] for d in AWAY[:-1]])[0]
    for d in AWAY:
        for yy in (y, 1 - y):
            if yy is y and d == 0 or yy is not y and d in FAR:
                continue
            send(att_s.at[chip], att_s.at[chip], TO_CHIPS, brsem.at[chip], ctx=at_chip(d, yy))
    for d in FAR:
        source = 2 * near(d) + y
        arrived(att_s.at[source], brsem.at[source])
        send(att_s.at[source], att_s.at[source], TO_CHIPS, brsem.at[source], ctx=ypeer)

    loads[4].wait()
    arrived(w_s.at[1 - core], rsem.at[3])
    weight = w_s[...].reshape(WIDE, HEADS * HD)
    for d in (0, *AWAY[3:-1], *FAR):
        to = near(d)
        for source in (2 * to, 2 * to + 1) if d and d not in FAR else (2 * to + 1 - y,):
            arrived(att_s.at[source], brsem.at[source])
        pair = att_s[pl.ds(2 * to, 2)]
        attended = jnp.concatenate(
            [pair[:, ROWS * h : ROWS * (h + 1), :].reshape(TOKB, HD) for h in range(HEADS)], axis=1
        )
        projected = dot(attended, weight, ((1,), (1,)))
        ps_s[to] = projected.astype(BF16)

        @pl.when(to == e)
        def _(projected=projected):
            own_p[...] = projected

        @pl.when(to != e)
        def _(to=to):
            send(ps_s.at[to], pr_s.at[e], TO_EXP, prsem.at[0], ex=to)

    loads[3].wait()
    arrived(h_s.at[1 - core], rsem.at[2])
    my_tokens = jnp.where(iota((TOKB, HALF), 1) == iota((TOKB, HALF), 0) + TOKB * e, 1.0, 0.0).astype(BF16)
    before_attention = dot(my_tokens, h_s[...].reshape(WIDE, HALF), ((1,), (1,)))
    stream = own_p[...]
    arrived(pr_s.at[pl.ds(0, EN - 1)], prsem.at[0])
    for d in range(1, EN):
        source = (e + d) % EN
        stream = stream + pr_s[source].astype(F32)
    stream = stream + before_attention
    st_s[e] = stream.astype(BF16)
    for d in EXP_FAR:
        to = (e + d) % EN
        send(st_s.at[e], st_s.at[e], TO_EXP_ALL, prsem.at[1], ex=to)
    arrived(st_s.at[pl.ds(0, EN - 1)], prsem.at[1])

    rows = st_s[...].reshape(HALF, WIDE)

    xs_s[...] = dot(hot_s[1 - core], rows).astype(BF16)
    push(xs_s, xr_s, ssem.at[7], rsem.at[7], ctx=sib)
    mine = dot(hot_s[core], rows)
    arrived(xr_s, rsem.at[7])
    x_s[z, y] = (mine + xr_s[...].astype(F32)).astype(BF16)

    low_half = pl.ds(SQ, SQ)

    def x_low(d, yy):
        return x_s.at[near(d), yy, low_half, :]

    def x_top(d, part):
        return x_s.at[near(d), :, pl.ds(PART * part, PART), :]

    def x_one(d, yy, part):
        return x_s.at[near(d), yy, pl.ds(PART * part, PART), :]

    FR, FL, OY = 0, PARTS, 2 * PARTS
    TR = [3 * PARTS + 3 * part for part in range(PARTS)]
    TL = [6 * PARTS + 2 * part for part in range(PARTS)]
    LR, LL = 8 * PARTS, 8 * PARTS + 3

    def same(block, kind, recv, to):
        send(block, block, kind, recv, ctx=to)

    def first_hops(part, base, d):
        for yy in (y, 1 - y):
            same(x_one(0, y, part), TO_FIRST, xrsem.at[base + part], at_chip(d, yy))

    same(x_low(0, y), TO_LOW, xrsem.at[LL], left)
    for part in range(PARTS):
        first_hops(part, FR, 1)
        first_hops(part, FL, -1)
    same(x_low(0, y), TO_LOW, xrsem.at[LR], right)
    same(x_low(0, y), TO_LOW_Y, trsem.at[z], ypeer)
    for part in range(PARTS):
        same(x_one(0, y, part), TO_FIRST, xrsem.at[OY + part], ypeer)

    resid = st_s[pl.ds(2 * (e % 4), 2)].reshape(OUTR, WIDE)
    take_own = jnp.where(iota((WIDE, 256), 0) == iota((WIDE, 256), 1) + COLS * core, 1.0, 0.0)
    take_sib = jnp.where(iota((WIDE, 256), 0) == iota((WIDE, 256), 1) + COLS * (1 - core), 1.0, 0.0)
    valid = iota((WIDE, 256), 1) < COLS
    take_s[0] = jnp.where(valid, take_own, 0.0).astype(BF16)
    take_s[1] = jnp.where(valid, take_sib, 0.0).astype(BF16)
    rs_s[...] = dot(resid, take_s[1]).astype(BF16)
    push(rs_s, rr_s, ssem.at[8], rsem.at[8], ctx=sib)
    ro_s[...] = dot(resid, take_s[0])

    loads[5].wait()
    loads[6].wait()
    loads[10].wait()
    arrived(gate_s.at[1 - core], rsem.at[4])
    arrived(up_s.at[1 - core], rsem.at[5])
    acc_s[...] = jnp.zeros_like(acc_s)
    sq_s[...] = jnp.zeros_like(sq_s)

    def project(d):
        zz = near(d)
        for yy in range(2):
            at = pl.ds(pl.multiple_of(WIDE * (2 * zz + yy), WIDE), WIDE)
            block = x_s[zz, yy].astype(F32)
            square = block * block
            sq_s[...] += square[:, :128] + square[:, 128:256] + square[:, 256:]
            scaled = (block * gain_ref[:, at]).astype(BF16)
            for kk in range(2):
                acc_s[0, kk] += dot(scaled, gate_s[kk, at, :])
                acc_s[1, kk] += dot(scaled, up_s[kk, at, :])

    def low_arrived(d):
        arrived(x_low(d, 1 - y), trsem.at[near(d)])

    def top_on(d, s, part, first, base, last, to):
        arrived(x_top(d, part), xrsem.at[first + part if s == 1 else base[part] + s - 2])
        if s < last:
            same(x_top(d, part), TO_PAIRS, xrsem.at[base[part] + s - 1], to)

    def low_on(d, s, base, last, to):
        block = x_low(d, y)
        arrived(block, xrsem.at[base + s - 1])
        if s < last:
            same(block, TO_LOW, xrsem.at[base + s], to)
        if s <= 3:
            same(block, TO_LOW_Y, trsem.at[near(d)], ypeer)
        if d == 3:
            same(block, TO_LOW_Y, trsem.at[near(d)], at_chip(-1, 1 - y))

    for s in range(1, 5):
        low_on(s, s, LL, 4, left)
        for part in range(PARTS):
            top_on(-s, s, part, FR, TR, 4, right)
            if s <= 3:
                top_on(s, s, part, FL, TL, 3, left)
        if s <= 3:
            low_on(-s, s, LR, 3, right)
        if s == 1:
            for part in range(PARTS):
                arrived(x_one(0, 1 - y, part), xrsem.at[OY + part])
            low_arrived(0)
            project(0)
        else:
            low_arrived(s - 1)
            project(s - 1)
            low_arrived(1 - s)
            project(1 - s)
    low_arrived(4)
    project(4)

    inverse_rms = lax.rsqrt(jnp.sum(sq_s[...], axis=1, keepdims=True) / D + 1e-5)
    hidden = []
    for kk in range(2):
        gate_val = acc_s[0, kk] * inverse_rms
        up_val = acc_s[1, kk] * inverse_rms
        hidden.append((gate_val / (1.0 + jnp.exp(-gate_val)) * up_val).astype(BF16))
    loads[7].wait()
    arrived(down_s.at[1 - core], rsem.at[6])

    def expand(d):
        zz = near(d)
        for yy in range(2):
            at = pl.ds(pl.multiple_of(WIDE * (2 * zz + yy), WIDE), WIDE)
            part_s[zz, yy] = dot(hidden[0], down_s[0, :, at]) + dot(hidden[1], down_s[1, :, at])
        if d == 0:
            f1s[...] = part_s[zz, 1 - y, :SQ, :].astype(BF16)
            push(f1s, f1r, ssem.at[9], rsem.at[9], ctx=ypeer)
        if d != 4:
            ys_s[zz] = part_s[zz, 1 - y, SQ:, :].astype(BF16)
            send(ys_s.at[zz], yr_s.at[zz], TO_SUM_Y, yrsem.at[zz], ctx=ypeer)

    LR, LL = 7 * PARTS, 7 * PARTS + 3

    def top_step(d, s, last, part, out_s, in_s, kind, base, step):
        value = part_s[near(d), :, PART * part : PART * (part + 1), :]
        if s:
            arrived(in_s.at[s - 1, part], ersem.at[base + s - 1])
            value = value + in_s[s - 1, part].astype(F32)
        out_s[s, part] = value.astype(BF16)
        if s < last:
            send(out_s.at[s, part], in_s.at[s, part], kind, ersem.at[base + s], ctx=at_chip(step, y))
        else:
            for yy in (y, 1 - y):
                send(out_s.at[s, part, yy], in_s.at[s, part, y], kind, ersem.at[base + s], ctx=at_chip(step, yy))

    def top_right(s):
        for part in range(PARTS):
            top_step(4 - s, s, 3, part, h1rs, h1rr, TO_TR, 4 * part, 1)

    def top_left(s):
        for part in range(PARTS):
            top_step(s - 3, s, 2, part, h1ls, h1lr, TO_TL, 4 * PARTS + 3 * part, -1)

    def low_value(d):
        arrived(yr_s.at[near(d)], yrsem.at[near(d)])
        return part_s[near(d), y, SQ:, :] + yr_s[near(d)].astype(F32)

    def low_right(s):
        value = low_value(3 - s)
        if s:
            arrived(h2rr.at[s - 1], ersem.at[LR + s - 1])
            value = value + h2rr[s - 1].astype(F32)
        h2rs[s] = value.astype(BF16)
        send(h2rs.at[s], h2rr.at[s], TO_LR, ersem.at[LR + s], ctx=right)

    def low_left(s):
        if s == 0:
            h2fs[...] = part_s[near(4), :, SQ:, :].astype(BF16)
            for yy in (y, 1 - y):
                send(h2fs.at[yy], h2fr.at[y], TO_LF, ersem.at[LL], ctx=at_chip(-1, yy))
            return
        value = low_value(s - 4)
        if s == 1:
            arrived(h2fr, ersem.at[LL])
            value = value + (h2fr[0].astype(F32) + h2fr[1].astype(F32))
        else:
            arrived(h2lr.at[s - 2], ersem.at[LL + s - 1])
            value = value + h2lr[s - 2].astype(F32)
        h2ls[s - 1] = value.astype(BF16)
        send(h2ls.at[s - 1], h2lr.at[s - 1], TO_LL, ersem.at[LL + s], ctx=left)

    expand(4)
    top_right(0)
    low_left(0)
    expand(3)
    expand(-3)
    top_left(0)
    for d in (-2, 2, -1, 1):
        expand(d)
    for s in range(1, 4):
        top_right(s)
        low_right(s - 1)
        low_left(s)
        if s < 3:
            top_left(s)
        if s == 2:
            expand(0)
    arrived(f1r, rsem.at[9])
    top_sum = part_s[z, y, :SQ, :] + f1r[...].astype(F32)
    ends = []
    for part in range(PARTS):
        end = top_sum[PART * part : PART * (part + 1)]
        arrived(h1rr.at[3, part], ersem.at[4 * part + 3])
        arrived(h1lr.at[2, part], ersem.at[4 * PARTS + 3 * part + 2])
        for yy in range(2):
            end = end + (h1rr[3, part, yy].astype(F32) + h1lr[2, part, yy].astype(F32))
        ends.append(end)
    low_sum = low_value(0)
    arrived(h2rr.at[2], ersem.at[LR + 2])
    arrived(h2lr.at[2], ersem.at[LL + 3])
    low_sum = low_sum + (h2rr[2].astype(F32) + h2lr[2].astype(F32))
    summed = (jnp.concatenate([*ends, low_sum], axis=0) * w_slot).astype(BF16)

    os_s[...] = dot(summed, take_s[1]).astype(BF16)
    push(os_s, or_s, ssem.at[10], rsem.at[10], ctx=sib)
    own_cols = dot(summed, take_s[0]).astype(BF16)
    arrived(or_s, rsem.at[10])
    o_s[core] = own_cols
    o_s[1 - core] = or_s[...]
    slots = o_s[...].reshape(SLOTS, 256)
    terms = dot(tok_s[...], slots).reshape(EN, OUTR, 256)
    tails = pltpu.roll(terms[:, TOKB:, HD:].reshape(HALF, HD), 64, 1).reshape(EN, TOKB, HD)
    terms = jnp.concatenate([terms[:, :, :HD], terms[:, :TOKB, HD:] + tails], axis=1)
    town_s[...] = terms
    ts_s[...] = terms.astype(BF16)
    for d in EXP_FAR:
        to = (e + d) % EN
        send(ts_s.at[to], tr_s.at[e], TO_TOK, prsem.at[2], ex=to)
    arrived(rr_s, rsem.at[8])
    resid = jnp.where(core == e // 4, ro_s[...], rr_s[...].astype(F32))
    mixed = town_s[e]
    arrived(tr_s.at[pl.ds(0, EN - 1)], prsem.at[2])
    for d in range(1, EN):
        mixed = mixed + tr_s[(e + d) % EN].astype(F32)
    tail = mixed[OUTR:]
    tail = jnp.concatenate([tail, pltpu.roll(tail, 64, 1)], axis=0)
    mixed = jnp.concatenate([mixed[:OUTR], tail], axis=1) + resid
    out_ref[...] = mixed[:, :COLS].astype(BF16)
    for copy in sent:
        copy.wait_send()
    for ref, kind in (
        (sib_s, TO_SIB), (num_s.at[pl.ds(0, ZN)], TO_Y), (num_s.at[pl.ds(ZN, ZN - 1)], TO_Z),
        (att_s.at[pl.ds(0, CHIPS - 1)], TO_CHIPS), (ps_s.at[pl.ds(0, EN - 1)], TO_EXP),
        (st_s.at[pl.ds(0, EN - 1)], TO_EXP_ALL), (x_s.at[:, 0, low_half, :], TO_LOW_Y),
        (x_s.at[pl.ds(0, 5), 0, low_half, :], TO_FIRST), (x_s.at[pl.ds(0, 5), 0], TO_PAIRS),
        (x_s.at[pl.ds(0, 7), 0, low_half, :], TO_LOW), (ys_s.at[pl.ds(0, ZN - 1)], TO_SUM_Y),
        (h1rs, TO_TR), (h1ls, TO_TL), (h2rs, TO_LR), (h2fs, TO_LF), (h2ls, TO_LL),
        (ts_s.at[pl.ds(0, EN - 1)], TO_TOK),
    ):
        left_here(ref, kind)


def local(hidden_in, queries, keys, values, out_weight, norm_gain, expert_gate, expert_up, expert_down, expert_ids, route_weights):
    vmem = pl.BlockSpec(memory_space=pltpu.VMEM)
    anywhere = pl.BlockSpec(memory_space=pltpu.HBM)
    dma = pltpu.SemaphoreType.DMA

    def buf(*shape, dtype=BF16):
        return pltpu.VMEM(shape, dtype)

    scratch = [
        buf(2, Q, dtype=jnp.int32), buf(2, Q, dtype=F32), buf(1, D, dtype=F32),
        buf(Q, HEADS * HD), buf(BLK, HD), buf(BLK, HD), buf(2, COLS, HALF),
        buf(2, COLS, HEADS * HD),
        buf(2, D, FF), buf(2, D, FF), buf(2, FF, D),
        buf(CHIPS, MSG, HD), buf(CHIPS, MSG, HD), buf(CHIPS, MSG, HD),
        buf(ZN, MSG, HD), buf(CHIPS, MSG, HD), buf(ZN, MSG, HD), buf(MSG, HD), buf(CHIPS, PAIRS, HD),
        buf(EN, TOKB, WIDE), buf(EN, TOKB, WIDE), buf(TOKB, WIDE, dtype=F32), buf(EN, TOKB, WIDE),
        buf(SH, WIDE), buf(SH, WIDE), buf(ZN, 2, SH, WIDE),
        buf(2, 2, SH, FF, dtype=F32), buf(SH, 128, dtype=F32), buf(ZN, 2, SH, WIDE, dtype=F32),
        buf(ZN, SQ, WIDE), buf(ZN, SQ, WIDE),
        buf(4, PARTS, 2, PART, WIDE), buf(4, PARTS, 2, PART, WIDE), buf(3, PARTS, 2, PART, WIDE), buf(3, PARTS, 2, PART, WIDE),
        buf(3, SQ, WIDE), buf(3, SQ, WIDE), buf(3, SQ, WIDE), buf(3, SQ, WIDE),
        buf(2, SQ, WIDE), buf(2, SQ, WIDE), buf(SQ, WIDE), buf(SQ, WIDE),
        buf(2, SH, 256), buf(SH, 256), buf(SH, 256), buf(2, SH, HALF), buf(2, WIDE, 256), buf(OUTR, 256, dtype=F32), buf(OUTR, 256), buf(OUTR, 256),
        buf(EN, PACK, HD), buf(EN, PACK, HD), buf(EN, PACK, HD, dtype=F32), buf(Q, SLOTS),
        dma((11,)), dma((11,)), dma((11,)), dma((17,)), dma((4,)), dma((ZN,)), dma((1,)), dma((CHIPS,)),
        dma((3,)), dma((ZN,)), dma((ZN,)), dma((8 * PARTS + 7,)), dma((7 * PARTS + 7,)),
    ]
    return pl.pallas_call(
        layer_kernel,
        out_shape=jax.ShapeDtypeStruct((OUTR, COLS), BF16),
        in_specs=[anywhere] * 11,
        out_specs=vmem,
        scratch_shapes=scratch,
        compiler_params=pltpu.CompilerParams(
            collective_id=0, has_side_effects=True, vmem_limit_bytes=40 * 1024 * 1024
        ),
        cost_estimate=pl.CostEstimate(flops=3 * 10**9, bytes_accessed=12 * 10**6, transcendentals=2 * 10**6),
    )(
        *(
            pltpu.with_memory_space_constraint(x, pltpu.HBM)
            for x in (
                expert_ids.T, route_weights.T, norm_gain.reshape(1, D), queries, keys, values, hidden_in.T,
                out_weight.T, expert_gate, expert_up, expert_down,
            )
        )
    )


def solution(mesh):
    placed = (
        P(None, "ctx"),
        P(None, "exp"),
        P("ctx", "exp"),
        P("ctx", "exp"),
        P("exp", "ctx"),
        P(),
        P("exp", None, "ctx"),
        P("exp", None, "ctx"),
        P("exp", "ctx", None),
        P(),
        P(),
    )
    return jax.shard_map(
        local, mesh=mesh, in_specs=placed, out_specs=P("exp", "ctx"), check_vma=False
    )
```

```python
import functools
import math

import jax
import jax.numpy as jnp
from jax import lax
from jax.experimental import pallas as pl
from jax.experimental.pallas import tpu as pltpu
from jax.sharding import PartitionSpec as P

F32 = jnp.float32
BF16 = jnp.bfloat16
MESH = pl.DeviceIdType.MESH

HD = 128
D = 6144
Q = 512
CONTEXT = 16384
CHIPS = 16
ZN = 8
EN = 8
HEADS = 6
HALF = Q // 2
ROWS = HALF // CHIPS
PAIRS = ROWS * HEADS
BLK = 512
WIDE = 384
COLS = 192
SLOTS = 256
SH = SLOTS // 2
SQ = SH // 2
TOKB = HALF // EN
OUTR = Q // EN
FF = 256
PACK = OUTR + OUTR // 2
MSG = PAIRS + 16
EXP_FAR = (5, 3, 7, 1, 4, 2, 6)
GROUP = 4
PARTS = 2
PART = SQ // PARTS
AWAY = (4, -3, 3, -2, 2, -1, 1, 0)
FAR = AWAY[:3]


def dot(a, b, dims=((1,), (0,))):
    return lax.dot_general(a, b, (dims, ((), ())), preferred_element_type=F32)


def iota(shape, dim):
    return lax.broadcasted_iota(jnp.int32, shape, dim)


def layer_kernel(
    ids_hbm, rw_hbm, gain_hbm, q_hbm, k_hbm, v_hbm, hin_hbm, wout_hbm, gate_hbm, up_hbm, down_hbm,
    out_ref,
    ids_ref, rw_ref, gain_ref, q_s, k_s, v_s, h_s, w_s, gate_s, up_s, down_s,
    sib_s, sibr_s, part_o, yin_s, num_s, got_s, own_s, att_s, ps_s, pr_s, own_p, st_s,
    xs_s, xr_s, x_s, acc_s, sq_s, part_s, ys_s, yr_s,
    h1rs, h1rr, h1ls, h1lr, h2rs, h2rr, h2ls, h2lr, h2fs, h2fr, f1s, f1r,
    o_s, os_s, or_s, hot_s, take_s, ro_s, rs_s, rr_s, ts_s, tr_s, town_s, tok_s,
    lsem, ssem, rsem, tosem, krsem, vrsem, arsem, brsem, prsem, trsem, yrsem, xrsem, ersem,
):
    c = lax.axis_index("ctx")
    e = lax.axis_index("exp")
    core = c % 2
    chip = c // 2
    y = chip % 2
    z = chip // 2
    sib = c + 1 - 2 * core
    ypeer = c + 2 - 4 * y
    zp = [(z + d) % ZN for d in range(ZN)]

    def near(d):
        return zp[d % ZN]

    def at_chip(d, yy):
        return near(d) * 4 + yy * 2 + core

    right, left = at_chip(1, y), at_chip(-1, y)

    def owner(i):
        return near(AWAY[i % ZN]) * 2 + (1 - y if i < ZN else y)

    def remote(src, dst, send, recv, ctx=None, ex=None):
        return pltpu.make_async_remote_copy(
            src_ref=src, dst_ref=dst, send_sem=send, recv_sem=recv,
            device_id=(c if ctx is None else ctx, e if ex is None else ex),
            device_id_type=MESH,
        )

    def arrived(ref, sem):
        pltpu.make_async_copy(ref, ref, sem).wait()

    sent = []

    def push(*args, **kw):
        copy = remote(*args, **kw)
        copy.start()
        sent.append(copy)

    (TO_SIB, TO_Y, TO_Z, TO_CHIPS, TO_EXP, TO_EXP_ALL, TO_LOW_Y, TO_FIRST, TO_PAIRS, TO_LOW, TO_SUM_Y,
     TO_TR, TO_TL, TO_LR, TO_LF, TO_LL, TO_TOK) = range(17)

    def send(src, dst, kind, recv, **kw):
        remote(src, dst, tosem.at[kind], recv, **kw).start()

    def left_here(ref, kind):
        remote(ref, ref, tosem.at[kind], tosem.at[kind], ctx=sib).wait_send()

    barrier = pltpu.get_barrier_semaphore()

    def greet(ctx, ex):
        pl.semaphore_signal(barrier, inc=1, device_id=(ctx, ex), device_id_type=MESH)

    greet(sib, e)
    for d in range(1, CHIPS):
        greet(2 * ((chip + d) % CHIPS) + core, e)
    for d in range(1, EN):
        greet(c, (e + d) % EN)

    half_cols = pl.ds(pl.multiple_of(HALF * core, HALF), HALF)
    sib_cols = pl.ds(pl.multiple_of(HALF * (1 - core), HALF), HALF)
    gate_h, up_h, down_h = gate_hbm.at[0], up_hbm.at[0], down_hbm.at[0]
    loads = [
        pltpu.make_async_copy(k_hbm, k_s, lsem.at[0]),
        pltpu.make_async_copy(q_hbm, q_s, lsem.at[1]),
        pltpu.make_async_copy(v_hbm, v_s, lsem.at[2]),
        pltpu.make_async_copy(hin_hbm.at[:, half_cols], h_s.at[core], lsem.at[3]),
        pltpu.make_async_copy(wout_hbm, w_s.at[core], lsem.at[4]),
        pltpu.make_async_copy(gate_h, gate_s.at[core], lsem.at[5]),
        pltpu.make_async_copy(up_h, up_s.at[core], lsem.at[6]),
        pltpu.make_async_copy(down_h, down_s.at[core], lsem.at[7]),
        pltpu.make_async_copy(ids_hbm, ids_ref, lsem.at[8]),
        pltpu.make_async_copy(rw_hbm, rw_ref, lsem.at[9]),
        pltpu.make_async_copy(gain_hbm, gain_ref, lsem.at[10]),
    ]
    for load in loads:
        load.start()

    loads[0].wait()
    loads[1].wait()
    loads[2].wait()
    keys = k_s[...]
    vals = jnp.concatenate([v_s[...], jnp.ones((BLK, HD), BF16)], axis=1)
    diag = iota((PAIRS, HD), 0) == iota((PAIRS, HD), 1)
    stat_row = iota((16, HD), 0)

    def stats_block(pk, tt):
        pk0 = pk.astype(BF16).astype(F32)
        pk1 = (pk - pk0).astype(BF16).astype(F32)
        tt0 = tt.astype(BF16).astype(F32)
        stats = jnp.where(stat_row == 0, pk0, 0.0)
        for at, term in ((1, pk1), (2, pk - pk0 - pk1), (3, tt0), (4, tt - tt0)):
            stats = jnp.where(stat_row == at, term, stats)
        return stats.astype(BF16)

    def stats_of(block):
        stats = block[PAIRS:, :].astype(F32)
        return stats[0:1] + stats[1:2] + stats[2:3], stats[3:4] + stats[4:5]

    def as_column(row):
        return jnp.sum(jnp.where(diag, row, 0.0), axis=1, keepdims=True)

    def attend(half, into, start):
        first_limit = CONTEXT - Q - BLK * c
        rows, limits = [], []
        for i in range(start, start + GROUP):
            first = HALF * half + ROWS * owner(i)
            at = pl.ds(pl.multiple_of(first, ROWS), ROWS)
            for h in range(HEADS):
                rows.append(q_s[at, HD * h : HD * (h + 1)])
                limits.append(iota((ROWS, 1), 0) + (first_limit + first))
        qg = jnp.concatenate(rows, axis=0)
        limit = jnp.concatenate(limits, axis=0)
        scores = dot(qg, keys, ((1,), (1,))) * (math.log2(math.e) / math.sqrt(HD))
        scores = jnp.where(iota(scores.shape, 1) <= limit, scores, -1e30)
        peak = jnp.max(scores, axis=1, keepdims=True)
        both = dot(jnp.exp2(scores - peak).astype(BF16), vals)
        total = both[:, HD:]
        numer = (both[:, :HD] / total).astype(BF16)
        peaks = jnp.broadcast_to(peak, total.shape)
        for g in range(GROUP):
            part = slice(PAIRS * g, PAIRS * (g + 1))
            pk = jnp.sum(jnp.where(diag, peaks[part], 0.0), axis=0, keepdims=True)
            tt = jnp.sum(jnp.where(diag, total[part], 0.0), axis=0, keepdims=True)
            into[start + g, :PAIRS, :] = numer[part]
            into[start + g, PAIRS:, :] = stats_block(pk, tt)

    for start in range(0, CHIPS, GROUP):
        attend(1 - core, sib_s, start)
    for start in range(0, CHIPS, GROUP):
        attend(core, part_o, start)

    pl.semaphore_wait(barrier, 1 + (CHIPS - 1) + (EN - 1))

    for g in range(CHIPS // GROUP):
        some = pl.ds(GROUP * g, GROUP)
        send(sib_s.at[some], sibr_s.at[some], TO_SIB, krsem.at[g], ctx=sib)
    push(hin_hbm.at[:, sib_cols], h_s.at[core], ssem.at[2], rsem.at[2], ctx=sib)
    push(wout_hbm, w_s.at[core], ssem.at[3], rsem.at[3], ctx=sib)
    push(gate_h, gate_s.at[core], ssem.at[4], rsem.at[4], ctx=sib)
    push(up_h, up_s.at[core], ssem.at[5], rsem.at[5], ctx=sib)
    push(down_h, down_s.at[core], ssem.at[6], rsem.at[6], ctx=sib)

    def merge(blocks):
        stats = [stats_of(block) for block in blocks]
        top = functools.reduce(jnp.maximum, [pk for pk, _ in stats])
        factors = [jnp.exp2(pk - top) * tt for pk, tt in stats]
        whole = sum(factors[1:], factors[0])
        inverse = 1.0 / jnp.maximum(whole, 1e-30)
        terms = [as_column(f * inverse) * block[:PAIRS, :].astype(F32) for f, block in zip(factors, blocks)]
        return sum(terms[1:], terms[0]).astype(BF16), top, whole

    def write(into, merged):
        numer, top, whole = merged
        into[:PAIRS, :] = numer
        into[PAIRS:, :] = stats_block(top, whole)

    def sibling_arrived(i):
        if i % GROUP == 0:
            arrived(sibr_s.at[pl.ds(i, GROUP)], krsem.at[i // GROUP])

    for i in range(ZN):
        sibling_arrived(i)
        write(num_s.at[i], merge([part_o.at[i], sibr_s.at[i]]))
        send(num_s.at[i], yin_s.at[i], TO_Y, vrsem.at[i], ctx=ypeer)
    for i in range(ZN):
        sibling_arrived(ZN + i)
        arrived(yin_s.at[i], vrsem.at[i])
        merged = merge([part_o.at[ZN + i], sibr_s.at[ZN + i], yin_s.at[i]])
        if AWAY[i]:
            write(num_s.at[ZN + i], merged)
            send(num_s.at[ZN + i], got_s.at[z], TO_Z, arsem.at[0], ctx=at_chip(AWAY[i], y))
        else:
            write(own_s, merged)

    loads[8].wait()
    loads[9].wait()
    ids = ids_ref[...]
    owned = jnp.where((ids[0:1] == e) | (ids[1:2] == e), 1.0, 0.0)
    w_row = jnp.where(ids[0:1] == e, rw_ref[0:1, :], 0.0) + jnp.where(ids[1:2] == e, rw_ref[1:2, :], 0.0)
    before = jnp.where(iota((Q, Q), 0) < iota((Q, Q), 1), 1.0, 0.0).astype(BF16)
    rank = dot(jnp.broadcast_to(owned, (16, Q)).astype(BF16), before)[0:1]
    place = jnp.where(owned > 0.5, rank, -1.0)
    place_col = jnp.transpose(jnp.broadcast_to(place, (HD, Q)))
    for part in range(2):
        lane = (iota((Q, SH), 1) + SH * part).astype(F32)
        tok_s[:, SH * part : SH * (part + 1)] = jnp.where(place_col == lane, 1.0, 0.0).astype(BF16)
    slot_own = (iota((SH, Q), 0) + SH * core).astype(F32)
    w_slot = jnp.sum(jnp.where(place == slot_own, w_row, 0.0), axis=1, keepdims=True)

    here = jnp.where(core == 0, place[:, :HALF], place[:, HALF:])
    for part in range(2):
        pick = (iota((SH, HALF), 0) + SH * part).astype(F32)
        hot_s[part] = jnp.where(here == pick, 1.0, 0.0).astype(BF16)

    arrived(got_s.at[pl.ds(0, ZN - 1)], arsem.at[0])
    att_s[chip] = merge([own_s] + [got_s.at[near(d)] for d in AWAY[:-1]])[0]
    for d in AWAY:
        for yy in (1 - y, y):
            if yy is y and d == 0 or yy is not y and d in FAR:
                continue
            send(att_s.at[chip], att_s.at[chip], TO_CHIPS, brsem.at[chip], ctx=at_chip(d, yy))
    for d in FAR:
        source = 2 * near(d) + y
        arrived(att_s.at[source], brsem.at[source])
        send(att_s.at[source], att_s.at[source], TO_CHIPS, brsem.at[source], ctx=ypeer)

    loads[4].wait()
    arrived(w_s.at[1 - core], rsem.at[3])
    weight = w_s[...].reshape(WIDE, HEADS * HD)
    for d in (0, *AWAY[3:-1], *FAR):
        to = near(d)
        for source in (2 * to, 2 * to + 1) if d and d not in FAR else (2 * to + 1 - y,):
            arrived(att_s.at[source], brsem.at[source])
        pair = att_s[pl.ds(2 * to, 2)]
        attended = jnp.concatenate(
            [pair[:, ROWS * h : ROWS * (h + 1), :].reshape(TOKB, HD) for h in range(HEADS)], axis=1
        )
        projected = dot(attended, weight, ((1,), (1,)))
        ps_s[to] = projected.astype(BF16)

        @pl.when(to == e)
        def _(projected=projected):
            own_p[...] = projected

        @pl.when(to != e)
        def _(to=to):
            send(ps_s.at[to], pr_s.at[e], TO_EXP, prsem.at[0], ex=to)

    loads[3].wait()
    arrived(h_s.at[1 - core], rsem.at[2])
    my_tokens = jnp.where(iota((TOKB, HALF), 1) == iota((TOKB, HALF), 0) + TOKB * e, 1.0, 0.0).astype(BF16)
    before_attention = dot(my_tokens, h_s[...].reshape(WIDE, HALF), ((1,), (1,)))
    stream = own_p[...]
    arrived(pr_s.at[pl.ds(0, EN - 1)], prsem.at[0])
    for d in range(1, EN):
        source = (e + d) % EN
        stream = stream + pr_s[source].astype(F32)
    stream = stream + before_attention
    st_s[e] = stream.astype(BF16)
    for d in EXP_FAR:
        to = (e + d) % EN
        send(st_s.at[e], st_s.at[e], TO_EXP_ALL, prsem.at[1], ex=to)
    arrived(st_s.at[pl.ds(0, EN - 1)], prsem.at[1])

    rows = st_s[...].reshape(HALF, WIDE)

    xs_s[...] = dot(hot_s[1 - core], rows).astype(BF16)
    push(xs_s, xr_s, ssem.at[7], rsem.at[7], ctx=sib)
    mine = dot(hot_s[core], rows)
    arrived(xr_s, rsem.at[7])
    x_s[z, y] = (mine + xr_s[...].astype(F32)).astype(BF16)

    low_half = pl.ds(SQ, SQ)

    def x_low(d, yy):
        return x_s.at[near(d), yy, low_half, :]

    def x_top(d, part):
        return x_s.at[near(d), :, pl.ds(PART * part, PART), :]

    def x_one(d, yy, part):
        return x_s.at[near(d), yy, pl.ds(PART * part, PART), :]

    FR, FL, OY = 0, PARTS, 2 * PARTS
    TR = [3 * PARTS + 3 * part for part in range(PARTS)]
    TL = [6 * PARTS + 2 * part for part in range(PARTS)]
    LR, LL = 8 * PARTS, 8 * PARTS + 3

    def same(block, kind, recv, to):
        send(block, block, kind, recv, ctx=to)

    def first_hops(part, base, d):
        for yy in (1 - y, y):
            same(x_one(0, y, part), TO_FIRST, xrsem.at[base + part], at_chip(d, yy))

    same(x_low(0, y), TO_LOW, xrsem.at[LL], left)
    for part in range(PARTS):
        first_hops(part, FR, 1)
        first_hops(part, FL, -1)
    same(x_low(0, y), TO_LOW, xrsem.at[LR], right)
    same(x_low(0, y), TO_LOW_Y, trsem.at[z], ypeer)
    for part in range(PARTS):
        same(x_one(0, y, part), TO_FIRST, xrsem.at[OY + part], ypeer)

    resid = st_s[pl.ds(2 * (e % 4), 2)].reshape(OUTR, WIDE)
    take_own = jnp.where(iota((WIDE, 256), 0) == iota((WIDE, 256), 1) + COLS * core, 1.0, 0.0)
    take_sib = jnp.where(iota((WIDE, 256), 0) == iota((WIDE, 256), 1) + COLS * (1 - core), 1.0, 0.0)
    valid = iota((WIDE, 256), 1) < COLS
    take_s[0] = jnp.where(valid, take_own, 0.0).astype(BF16)
    take_s[1] = jnp.where(valid, take_sib, 0.0).astype(BF16)
    rs_s[...] = dot(resid, take_s[1]).astype(BF16)
    push(rs_s, rr_s, ssem.at[8], rsem.at[8], ctx=sib)
    ro_s[...] = dot(resid, take_s[0])

    loads[5].wait()
    loads[6].wait()
    loads[10].wait()
    arrived(gate_s.at[1 - core], rsem.at[4])
    arrived(up_s.at[1 - core], rsem.at[5])
    acc_s[...] = jnp.zeros_like(acc_s)
    sq_s[...] = jnp.zeros_like(sq_s)

    def project(d):
        zz = near(d)
        for yy in range(2):
            at = pl.ds(pl.multiple_of(WIDE * (2 * zz + yy), WIDE), WIDE)
            block = x_s[zz, yy].astype(F32)
            square = block * block
            sq_s[...] += square[:, :128] + square[:, 128:256] + square[:, 256:]
            scaled = (block * gain_ref[:, at]).astype(BF16)
            for kk in range(2):
                acc_s[0, kk] += dot(scaled, gate_s[kk, at, :])
                acc_s[1, kk] += dot(scaled, up_s[kk, at, :])

    def low_arrived(d):
        arrived(x_low(d, 1 - y), trsem.at[near(d)])

    def top_on(d, s, part, first, base, last, to):
        arrived(x_top(d, part), xrsem.at[first + part if s == 1 else base[part] + s - 2])
        if s < last:
            same(x_top(d, part), TO_PAIRS, xrsem.at[base[part] + s - 1], to)

    def low_on(d, s, base, last, to):
        block = x_low(d, y)
        arrived(block, xrsem.at[base + s - 1])
        if s < last:
            same(block, TO_LOW, xrsem.at[base + s], to)
        if s <= 3:
            same(block, TO_LOW_Y, trsem.at[near(d)], ypeer)
        if d == 3:
            same(block, TO_LOW_Y, trsem.at[near(d)], at_chip(-1, 1 - y))

    for s in range(1, 5):
        low_on(s, s, LL, 4, left)
        for part in range(PARTS):
            top_on(-s, s, part, FR, TR, 4, right)
            if s <= 3:
                top_on(s, s, part, FL, TL, 3, left)
        if s <= 3:
            low_on(-s, s, LR, 3, right)
        if s == 1:
            for part in range(PARTS):
                arrived(x_one(0, 1 - y, part), xrsem.at[OY + part])
            low_arrived(0)
            project(0)
        else:
            low_arrived(s - 1)
            project(s - 1)
            low_arrived(1 - s)
            project(1 - s)
    low_arrived(4)
    project(4)

    inverse_rms = lax.rsqrt(jnp.sum(sq_s[...], axis=1, keepdims=True) / D + 1e-5)
    hidden = []
    for kk in range(2):
        gate_val = acc_s[0, kk] * inverse_rms
        up_val = acc_s[1, kk] * inverse_rms
        hidden.append((gate_val / (1.0 + jnp.exp(-gate_val)) * up_val).astype(BF16))
    loads[7].wait()
    arrived(down_s.at[1 - core], rsem.at[6])

    def expand(d):
        zz = near(d)
        for yy in range(2):
            at = pl.ds(pl.multiple_of(WIDE * (2 * zz + yy), WIDE), WIDE)
            part_s[zz, yy] = dot(hidden[0], down_s[0, :, at]) + dot(hidden[1], down_s[1, :, at])
        if d == 0:
            f1s[...] = part_s[zz, 1 - y, :SQ, :].astype(BF16)
            push(f1s, f1r, ssem.at[9], rsem.at[9], ctx=ypeer)
        if d != 4:
            ys_s[zz] = part_s[zz, 1 - y, SQ:, :].astype(BF16)
            send(ys_s.at[zz], yr_s.at[zz], TO_SUM_Y, yrsem.at[zz], ctx=ypeer)

    LR, LL = 7 * PARTS, 7 * PARTS + 3

    def top_step(d, s, last, part, out_s, in_s, kind, base, step):
        value = part_s[near(d), :, PART * part : PART * (part + 1), :]
        if s:
            arrived(in_s.at[s - 1, part], ersem.at[base + s - 1])
            value = value + in_s[s - 1, part].astype(F32)
        out_s[s, part] = value.astype(BF16)
        if s < last:
            send(out_s.at[s, part], in_s.at[s, part], kind, ersem.at[base + s], ctx=at_chip(step, y))
        else:
            for yy in (1 - y, y):
                send(out_s.at[s, part, yy], in_s.at[s, part, y], kind, ersem.at[base + s], ctx=at_chip(step, yy))

    def top_right(s):
        for part in range(PARTS):
            top_step(4 - s, s, 3, part, h1rs, h1rr, TO_TR, 4 * part, 1)

    def top_left(s):
        for part in range(PARTS):
            top_step(s - 3, s, 2, part, h1ls, h1lr, TO_TL, 4 * PARTS + 3 * part, -1)

    def low_value(d):
        arrived(yr_s.at[near(d)], yrsem.at[near(d)])
        return part_s[near(d), y, SQ:, :] + yr_s[near(d)].astype(F32)

    def low_right(s):
        value = low_value(3 - s)
        if s:
            arrived(h2rr.at[s - 1], ersem.at[LR + s - 1])
            value = value + h2rr[s - 1].astype(F32)
        h2rs[s] = value.astype(BF16)
        send(h2rs.at[s], h2rr.at[s], TO_LR, ersem.at[LR + s], ctx=right)

    def low_left(s):
        if s == 0:
            h2fs[...] = part_s[near(4), :, SQ:, :].astype(BF16)
            for yy in (1 - y, y):
                send(h2fs.at[yy], h2fr.at[y], TO_LF, ersem.at[LL], ctx=at_chip(-1, yy))
            return
        value = low_value(s - 4)
        if s == 1:
            arrived(h2fr, ersem.at[LL])
            value = value + (h2fr[0].astype(F32) + h2fr[1].astype(F32))
        else:
            arrived(h2lr.at[s - 2], ersem.at[LL + s - 1])
            value = value + h2lr[s - 2].astype(F32)
        h2ls[s - 1] = value.astype(BF16)
        send(h2ls.at[s - 1], h2lr.at[s - 1], TO_LL, ersem.at[LL + s], ctx=left)

    expand(4)
    top_right(0)
    low_left(0)
    expand(3)
    expand(-3)
    top_left(0)
    for d in (-2, 2, -1, 1):
        expand(d)
    for s in range(1, 4):
        top_right(s)
        low_right(s - 1)
        low_left(s)
        if s < 3:
            top_left(s)
        if s == 2:
            expand(0)
    arrived(f1r, rsem.at[9])
    top_sum = part_s[z, y, :SQ, :] + f1r[...].astype(F32)
    ends = []
    for part in range(PARTS):
        end = top_sum[PART * part : PART * (part + 1)]
        arrived(h1rr.at[3, part], ersem.at[4 * part + 3])
        arrived(h1lr.at[2, part], ersem.at[4 * PARTS + 3 * part + 2])
        for yy in range(2):
            end = end + (h1rr[3, part, yy].astype(F32) + h1lr[2, part, yy].astype(F32))
        ends.append(end)
    low_sum = low_value(0)
    arrived(h2rr.at[2], ersem.at[LR + 2])
    arrived(h2lr.at[2], ersem.at[LL + 3])
    low_sum = low_sum + (h2rr[2].astype(F32) + h2lr[2].astype(F32))
    summed = (jnp.concatenate([*ends, low_sum], axis=0) * w_slot).astype(BF16)

    os_s[...] = dot(summed, take_s[1]).astype(BF16)
    push(os_s, or_s, ssem.at[10], rsem.at[10], ctx=sib)
    own_cols = dot(summed, take_s[0]).astype(BF16)
    arrived(or_s, rsem.at[10])
    o_s[core] = own_cols
    o_s[1 - core] = or_s[...]
    slots = o_s[...].reshape(SLOTS, 256)
    terms = dot(tok_s[...], slots).reshape(EN, OUTR, 256)
    tails = pltpu.roll(terms[:, TOKB:, HD:].reshape(HALF, HD), 64, 1).reshape(EN, TOKB, HD)
    terms = jnp.concatenate([terms[:, :, :HD], terms[:, :TOKB, HD:] + tails], axis=1)
    town_s[...] = terms
    ts_s[...] = terms.astype(BF16)
    for d in EXP_FAR:
        to = (e + d) % EN
        send(ts_s.at[to], tr_s.at[e], TO_TOK, prsem.at[2], ex=to)
    arrived(rr_s, rsem.at[8])
    resid = jnp.where(core == e // 4, ro_s[...], rr_s[...].astype(F32))
    mixed = town_s[e]
    arrived(tr_s.at[pl.ds(0, EN - 1)], prsem.at[2])
    for d in range(1, EN):
        mixed = mixed + tr_s[(e + d) % EN].astype(F32)
    tail = mixed[OUTR:]
    tail = jnp.concatenate([tail, pltpu.roll(tail, 64, 1)], axis=0)
    mixed = jnp.concatenate([mixed[:OUTR], tail], axis=1) + resid
    out_ref[...] = mixed[:, :COLS].astype(BF16)
    for copy in sent:
        copy.wait_send()
    for ref, kind in (
        (sib_s, TO_SIB), (num_s.at[pl.ds(0, ZN)], TO_Y), (num_s.at[pl.ds(ZN, ZN - 1)], TO_Z),
        (att_s.at[pl.ds(0, CHIPS - 1)], TO_CHIPS), (ps_s.at[pl.ds(0, EN - 1)], TO_EXP),
        (st_s.at[pl.ds(0, EN - 1)], TO_EXP_ALL), (x_s.at[:, 0, low_half, :], TO_LOW_Y),
        (x_s.at[pl.ds(0, 5), 0, low_half, :], TO_FIRST), (x_s.at[pl.ds(0, 5), 0], TO_PAIRS),
        (x_s.at[pl.ds(0, 7), 0, low_half, :], TO_LOW), (ys_s.at[pl.ds(0, ZN - 1)], TO_SUM_Y),
        (h1rs, TO_TR), (h1ls, TO_TL), (h2rs, TO_LR), (h2fs, TO_LF), (h2ls, TO_LL),
        (ts_s.at[pl.ds(0, EN - 1)], TO_TOK),
    ):
        left_here(ref, kind)


def local(hidden_in, queries, keys, values, out_weight, norm_gain, expert_gate, expert_up, expert_down, expert_ids, route_weights):
    vmem = pl.BlockSpec(memory_space=pltpu.VMEM)
    anywhere = pl.BlockSpec(memory_space=pltpu.HBM)
    dma = pltpu.SemaphoreType.DMA

    def buf(*shape, dtype=BF16):
        return pltpu.VMEM(shape, dtype)

    scratch = [
        buf(2, Q, dtype=jnp.int32), buf(2, Q, dtype=F32), buf(1, D, dtype=F32),
        buf(Q, HEADS * HD), buf(BLK, HD), buf(BLK, HD), buf(2, COLS, HALF),
        buf(2, COLS, HEADS * HD),
        buf(2, D, FF), buf(2, D, FF), buf(2, FF, D),
        buf(CHIPS, MSG, HD), buf(CHIPS, MSG, HD), buf(CHIPS, MSG, HD),
        buf(ZN, MSG, HD), buf(CHIPS, MSG, HD), buf(ZN, MSG, HD), buf(MSG, HD), buf(CHIPS, PAIRS, HD),
        buf(EN, TOKB, WIDE), buf(EN, TOKB, WIDE), buf(TOKB, WIDE, dtype=F32), buf(EN, TOKB, WIDE),
        buf(SH, WIDE), buf(SH, WIDE), buf(ZN, 2, SH, WIDE),
        buf(2, 2, SH, FF, dtype=F32), buf(SH, 128, dtype=F32), buf(ZN, 2, SH, WIDE, dtype=F32),
        buf(ZN, SQ, WIDE), buf(ZN, SQ, WIDE),
        buf(4, PARTS, 2, PART, WIDE), buf(4, PARTS, 2, PART, WIDE), buf(3, PARTS, 2, PART, WIDE), buf(3, PARTS, 2, PART, WIDE),
        buf(3, SQ, WIDE), buf(3, SQ, WIDE), buf(3, SQ, WIDE), buf(3, SQ, WIDE),
        buf(2, SQ, WIDE), buf(2, SQ, WIDE), buf(SQ, WIDE), buf(SQ, WIDE),
        buf(2, SH, 256), buf(SH, 256), buf(SH, 256), buf(2, SH, HALF), buf(2, WIDE, 256), buf(OUTR, 256, dtype=F32), buf(OUTR, 256), buf(OUTR, 256),
        buf(EN, PACK, HD), buf(EN, PACK, HD), buf(EN, PACK, HD, dtype=F32), buf(Q, SLOTS),
        dma((11,)), dma((11,)), dma((11,)), dma((17,)), dma((4,)), dma((ZN,)), dma((1,)), dma((CHIPS,)),
        dma((3,)), dma((ZN,)), dma((ZN,)), dma((8 * PARTS + 7,)), dma((7 * PARTS + 7,)),
    ]
    return pl.pallas_call(
        layer_kernel,
        out_shape=jax.ShapeDtypeStruct((OUTR, COLS), BF16),
        in_specs=[anywhere] * 11,
        out_specs=vmem,
        scratch_shapes=scratch,
        compiler_params=pltpu.CompilerParams(
            collective_id=0, has_side_effects=True, vmem_limit_bytes=40 * 1024 * 1024
        ),
        cost_estimate=pl.CostEstimate(flops=3 * 10**9, bytes_accessed=12 * 10**6, transcendentals=2 * 10**6),
    )(
        *(
            pltpu.with_memory_space_constraint(x, pltpu.HBM)
            for x in (
                expert_ids.T, route_weights.T, norm_gain.reshape(1, D), queries, keys, values, hidden_in.T,
                out_weight.T, expert_gate, expert_up, expert_down,
            )
        )
    )


def solution(mesh):
    placed = (
        P(None, "ctx"),
        P(None, "exp"),
        P("ctx", "exp"),
        P("ctx", "exp"),
        P("exp", "ctx"),
        P(),
        P("exp", None, "ctx"),
        P("exp", None, "ctx"),
        P("exp", "ctx", None),
        P(),
        P(),
    )
    return jax.shard_map(
        local, mesh=mesh, in_specs=placed, out_specs=P("exp", "ctx"), check_vma=False
    )
```
